512 devices in a mesh: rows: 64 (over y_hi, z, core), tp: 8 (over x, y_lo).
Axes of the slice: x: 4, y: 4 (y_hi: 2, y_lo: 2; y = y_hi * 2 + y_lo), z: 16, core: 2. Of those that a mesh axis runs over, the one named last changes fastest.
Arguments:
- resid: bfloat16 [49152, 8192], P('rows', 'tp'), may hold values from -41 to 41
- attention_heads_output: bfloat16 [49152, 8192], P('rows', 'tp'), may hold values from -6 to 6
- adapter_down_matrix: bfloat16 [8192, 64], P('tp'), may hold values from -0.0625 to 0.0625
- adapter_up_matrix: bfloat16 [64, 8192], P(None, 'tp'), may hold values from -0.75 to 0.75
- drafter_norm_scale: bfloat16 [8192], P('tp'), may hold values from 0.099609375 to 1.8984375
- drafter_value_matrix: bfloat16 [8192, 512], P('tp'), may hold values from -0.0625 to 0.0625
- target: bfloat16 [49152, 512], P(('rows', 'tp')), may hold values from -6 to 6
Outputs:
- values: bfloat16 [49152, 512], P(('rows', 'tp'))
- value_grad: bfloat16 [8192, 512], P(('tp', 'rows'))
- a_grad: float32 [8192, 64], P('tp')
- b_grad: float32 [64, 8192], P(None, 'tp')
- gain_grad: float32 [8192], P('tp')
The draws below stay inside these ranges and needn't reach their ends.
All inputs are finite; a program needn't handle non-finite values.
Results may differ from the reference program's by a relative error of at most 0.0052.
Values may be sent and summed in bfloat16 or wider, within the bound.
No kernel may reach another device: no remote copies, remote signals or barrier semaphores. Data moves between devices by JAX's collectives and lax.ppermute only.
A program may use at most 64 MiB of HBM per device.

```python
import math
import jax
import jax.numpy as jnp
from jax import lax

MODEL_WIDTH = 8192
ADAPTER_RANK = 64
KVW = 512
TOK_ROW = 768
TOKENS = 49152


def draw_resid(key, part):
    key = jax.random.fold_in(key, 7)
    noise_key, column_key = jax.random.split(key, 2)
    position = lax.iota(jnp.float32, MODEL_WIDTH) / (MODEL_WIDTH - 1)
    columns = jnp.exp(math.log(3.0) * position + jax.random.uniform(column_key, (MODEL_WIDTH,), jnp.float32, 0.0, math.log(2.0)))
    noise_field = jnp.clip(jax.random.normal(noise_key, (TOKENS, MODEL_WIDTH), jnp.float32), -4.0, 4.0)
    return (noise_field * columns).astype(jnp.bfloat16)


def block_levels(stream_key, shape, pieces, low, largest):
    def one(dim, blocks):
        heights = jax.random.uniform(jax.random.fold_in(jax.random.fold_in(stream_key, 6), dim), (blocks,), jnp.float32, low / len(pieces), largest / len(pieces))
        return jnp.repeat(jnp.exp(heights), shape[dim] // blocks).reshape((-1,) + (1,) * (len(shape) - dim - 1))

    gain = one(*pieces[0])
    for cut in pieces[1:]:
        gain = gain * one(*cut)
    return gain


def scatter_about(own_key, extent, deviation, bound, pieces=(), held_as=jnp.bfloat16):
    factor_of = block_levels(own_key, extent, pieces, -0.22, 0.18) if pieces else 1.0
    entries = jax.random.normal(own_key, extent, jnp.float32) * deviation * factor_of
    return jnp.minimum(jnp.maximum(entries, -bound), bound).astype(held_as)


def setup_inputs(seed: int = 0) -> dict:
    streams_of = jax.random.split(jax.random.key(seed), 8)
    return {
        "resid": draw_resid(jax.random.fold_in(streams_of[7], 71), 0),
        "attention_heads_output": scatter_about(streams_of[1], (TOKENS, MODEL_WIDTH), 1.0, 6.0, ((0, 64), (1, 8))),
        "adapter_down_matrix": scatter_about(streams_of[2], (MODEL_WIDTH, ADAPTER_RANK), MODEL_WIDTH ** -0.5, 0.0625, ((0, 8),)),
        "adapter_up_matrix": scatter_about(streams_of[3], (ADAPTER_RANK, MODEL_WIDTH), ADAPTER_RANK ** -0.5, 0.75, ((1, 8),)),
        "drafter_norm_scale": jnp.clip(1.0 + 0.18 * jax.random.normal(streams_of[4], (MODEL_WIDTH,), jnp.float32), 0.099609375, 1.8984375).astype(jnp.bfloat16),
        "drafter_value_matrix": scatter_about(streams_of[5], (MODEL_WIDTH, KVW), MODEL_WIDTH ** -0.5, 0.0625, ((0, 8),)),
        "target": scatter_about(streams_of[6], (TOKENS, KVW), 1.0, 6.0, ((0, 512),)),
    }


EPSILON = 1e-06

def reference(resid, attention_heads_output, adapter_down_matrix, adapter_up_matrix, drafter_norm_scale, drafter_value_matrix, target):
    loss_scale = 1.0 / TOKENS ** 0.5
    gain_wide = drafter_norm_scale.astype(jnp.float32)
    up_matrix_wide = adapter_up_matrix.astype(jnp.float32)
    contract_rows = (((0,), (0,)), ((), ()))

    def one_block(totals, block_index):
        first_row = (block_index * TOK_ROW).astype(jnp.int32)
        input_rows = lax.dynamic_slice_in_dim(resid, first_row, TOK_ROW, 0)
        head_rows = lax.dynamic_slice_in_dim(attention_heads_output, first_row, TOK_ROW, 0)
        wanted = lax.dynamic_slice_in_dim(target, first_row, TOK_ROW, 0)
        down_projected = jnp.dot(head_rows, adapter_down_matrix, preferred_element_type=jnp.float32)
        down_times_up = down_projected.astype(jnp.bfloat16)
        hidden_rows = input_rows.astype(jnp.float32) + 0.5 * jnp.dot(down_times_up, adapter_up_matrix, preferred_element_type=jnp.float32)
        inverse_rms = lax.rsqrt(lax.optimization_barrier(jnp.sum(hidden_rows * hidden_rows, axis=1)) / MODEL_WIDTH + EPSILON)
        normed = (hidden_rows * inverse_rms[:, None] * gain_wide).astype(jnp.bfloat16)
        sums = jnp.dot(normed, drafter_value_matrix, preferred_element_type=jnp.float32)
        value_error = ((sums - wanted.astype(jnp.float32)) * loss_scale).astype(jnp.bfloat16)
        value_part = lax.dot_general(normed, value_error, contract_rows, preferred_element_type=jnp.float32)
        normed_grad = lax.dot_general(value_error, drafter_value_matrix, (((1,), (1,)), ((), ())), preferred_element_type=jnp.float32)
        gain_part = lax.optimization_barrier(jnp.sum(normed_grad * hidden_rows * inverse_rms[:, None], axis=0))
        scaled_grad = normed_grad * gain_wide
        inner = lax.optimization_barrier(jnp.sum(scaled_grad * hidden_rows, axis=1))
        hidden_grad = inverse_rms[:, None] * scaled_grad - hidden_rows * (inner * inverse_rms ** 3 / MODEL_WIDTH)[:, None]
        down_grad = 0.5 * jnp.dot(hidden_grad, up_matrix_wide.T, precision=lax.Precision.HIGHEST)
        b_part = 0.5 * lax.dot_general(down_times_up.astype(jnp.float32), hidden_grad, contract_rows, precision=lax.Precision.HIGHEST)
        a_part = lax.dot_general(head_rows, down_grad.astype(jnp.bfloat16), contract_rows, preferred_element_type=jnp.float32)
        totals = (totals[0] + value_part, totals[1] + a_part, totals[2] + b_part, totals[3] + gain_part)
        return (totals, sums.astype(jnp.bfloat16))
    start = (jnp.zeros((MODEL_WIDTH, KVW), jnp.float32), jnp.zeros((MODEL_WIDTH, ADAPTER_RANK), jnp.float32), jnp.zeros((ADAPTER_RANK, MODEL_WIDTH), jnp.float32), jnp.zeros((MODEL_WIDTH,), jnp.float32))
    totals, values = lax.scan(one_block, start, jnp.arange(TOKENS // TOK_ROW, dtype=jnp.int32))
    return (values.reshape(TOKENS, KVW), totals[0].astype(jnp.bfloat16), totals[1], totals[2], totals[3])
```

```python
import jax
import jax.numpy as jnp
from jax import lax
from jax.sharding import Mesh, PartitionSpec as P

MODEL_WIDTH = 8192
EPSILON = 1e-06
TP = ("x", "y_lo")
ROWS = ("y_hi", "z", "core")
bf16 = jnp.bfloat16
f32 = jnp.float32


def dot(a, b, dims=(((1,), (0,)), ((), ()))):
    return lax.dot_general(a, b, dims, preferred_element_type=f32)


NT = (((1,), (1,)), ((), ()))
TN = (((0,), (0,)), ((), ()))


def split(x):
    high = lax.reduce_precision(x, 8, 7)
    return high.astype(bf16), (x - high).astype(bf16)


def dot_split(a, b, dims=(((1,), (0,)), ((), ()))):
    return dot(a, b[0], dims) + dot(a, b[1], dims)


def body(resid, heads, down_matrix, up, scale, value_matrix, target):
    share = target.shape[0]
    tp = resid.shape[0] // share
    tokens = resid.shape[0] * lax.axis_size(ROWS)
    loss_scale = 1.0 / tokens**0.5
    gain = scale.astype(f32)
    rank = up.shape[0]
    width = target.shape[1]

    up_high, up_low = split(up.astype(f32) * gain)
    weights = jnp.concatenate(
        [
            dot(up_high, value_matrix) + dot(up_low, value_matrix),
            dot(up, up, NT),
            jnp.zeros((rank, rank), f32),
        ],
        axis=1,
    )
    columns = weights.shape[1]

    wide = resid.astype(f32)
    part = jnp.concatenate(
        [
            dot((wide * gain).astype(bf16), value_matrix),
            dot(heads, down_matrix),
            dot(resid, up, NT),
        ],
        axis=1,
    )
    squares = jnp.sum(wide * wide, axis=1).reshape(tp, 1, share)
    tail = jnp.concatenate(split(squares), axis=1)
    tail = jnp.pad(tail, ((0, 0), (0, 14), (0, columns - share)))
    pieces = jnp.concatenate(
        [
            part.astype(bf16).reshape(tp, share, columns),
            jnp.broadcast_to(weights.astype(bf16), (tp, rank, columns)),
            tail,
        ],
        axis=1,
    )
    pieces = lax.all_to_all(pieces, TP, 0, 0, tiled=True)
    total = jnp.sum(pieces.astype(f32), axis=0)
    through = split(total[share : share + rank, :width])
    gram = split(total[share : share + rank, width : width + rank])
    square_sums = total[share + rank, :share] + total[share + rank + 1, :share]

    down_b = total[:share, width : width + rank].astype(bf16)
    down_wide = down_b.astype(f32)
    along = total[:share, width + rank :]
    hidden_up = along + 0.5 * dot_split(down_b, gram)
    square_sums = square_sums + 0.5 * jnp.sum(down_wide * (along + hidden_up), axis=1)
    inverse_rms = lax.rsqrt(square_sums / MODEL_WIDTH + EPSILON)[:, None]
    sums = inverse_rms * (total[:share, :width] + 0.5 * dot_split(down_b, through))
    error = ((sums - target.astype(f32)) * loss_scale).astype(bf16)
    error_wide = error.astype(f32)
    inner = jnp.sum(error_wide * sums, axis=1, keepdims=True) / MODEL_WIDTH
    down_grad = 0.5 * inverse_rms * (dot_split(error, through, NT) - inner * inverse_rms * hidden_up)
    sent = jnp.concatenate(
        [
            error_wide * inverse_rms,
            down_wide,
            down_grad,
            down_wide * (inner * inverse_rms * inverse_rms),
        ],
        axis=1,
    ).astype(bf16)
    every = lax.all_to_all(jnp.broadcast_to(sent, (tp, *sent.shape)), TP, 0, 0, tiled=True)
    every = every.reshape(tp * share, -1)

    error_all = every[:, :width]
    down_all = every[:, width : width + rank]
    grad_all = every[:, width + rank : width + 2 * rank]
    weighted_all = every[:, width + 2 * rank :]
    hidden = (wide + 0.5 * dot(down_all, up)).astype(bf16)
    value_part = dot(hidden, error_all, TN)
    a_part = dot(heads, grad_all, TN)
    cross = split(dot(error_all, down_all, TN))
    b_part = 0.5 * (gain[:, None] * dot_split(value_matrix, cross) - dot(hidden, weighted_all, TN))
    part = jnp.concatenate([value_part, a_part, b_part], axis=1)

    blocks = [lax.axis_size(a) for a in ROWS]
    own = part.shape[0] // (blocks[0] * blocks[1] * blocks[2])
    part = part.reshape(*blocks, own, columns)
    part = pair_sum(part, "core", 2)
    part = pair_sum(part, "y_hi", 0)
    part = lax.all_to_all(part.astype(bf16), "z", 0, 0, tiled=True)
    part = jnp.sum(part.astype(f32), axis=0)

    first = lax.axis_index(ROWS) * own
    own_gain = lax.dynamic_slice_in_dim(gain, first, own, 0)
    own_matrix = lax.dynamic_slice_in_dim(value_matrix, first, own, 0).astype(f32)
    value_grad = (part[:, :width] * own_gain[:, None]).astype(bf16)
    gain_part = jnp.sum(part[:, :width] * own_matrix, axis=1)

    small = jnp.concatenate(
        [part[:, width:], jnp.pad(gain_part[None, :], ((0, 7), (0, 2 * rank - own)))], axis=0
    )
    small = pair_gather(small, "y_hi")
    small = lax.all_to_all(
        jnp.broadcast_to(small, (blocks[1], *small.shape)), "z", 0, 0, tiled=True
    )
    small = pair_gather(small, "core")
    small = small.transpose(2, 1, 0, 3, 4)
    a_b = small[:, :, :, :own].reshape(-1, 2 * rank)
    gain_grad = small[:, :, :, own, :own].reshape(-1)
    return (sums.astype(bf16), value_grad, a_b[:, :rank], a_b[:, rank:].T, gain_grad)


def swap(x, axis):
    return lax.ppermute(x, axis, [(0, 1), (1, 0)])


def pair_sum(x, axis, dim):
    me = lax.axis_index(axis)
    mine = lax.dynamic_index_in_dim(x, me, dim, keepdims=False)
    other = lax.dynamic_index_in_dim(x, 1 - me, dim, keepdims=False)
    return mine.astype(f32) + swap(other.astype(bf16), axis).astype(f32)


def pair_gather(x, axis):
    me = lax.axis_index(axis)
    other = swap(x, axis)
    first = me == 0
    return jnp.stack([jnp.where(first, x, other), jnp.where(first, other, x)])


def solution(mesh):
    rows, tp = mesh.shape["rows"], mesh.shape["tp"]
    y_hi, core, y_lo = 2, 2, 2
    fine = Mesh(
        mesh.devices.reshape(y_hi, rows // (y_hi * core), core, tp // y_lo, y_lo), (*ROWS, *TP)
    )
    in_specs = (
        P(ROWS, TP),
        P(ROWS, TP),
        P(TP, None),
        P(None, TP),
        P(TP),
        P(TP, None),
        P((*ROWS, *TP), None),
    )
    out_specs = (
        P((*ROWS, *TP), None),
        P((*TP, *ROWS), None),
        P(TP, None),
        P(None, TP),
        P(TP),
    )
    return jax.shard_map(body, mesh=fine, in_specs=in_specs, out_specs=out_specs, check_vma=False)
```

```python
import jax
import jax.numpy as jnp
from jax import lax
from jax.sharding import Mesh, PartitionSpec as P

MODEL_WIDTH = 8192
EPSILON = 1e-06
TP = ("x", "y_lo")
ROWS = ("y_hi", "z", "core")
bf16 = jnp.bfloat16
f32 = jnp.float32


def dot(a, b, dims=(((1,), (0,)), ((), ()))):
    return lax.dot_general(a, b, dims, preferred_element_type=f32)


NT = (((1,), (1,)), ((), ()))
TN = (((0,), (0,)), ((), ()))


def split(x):
    high = lax.reduce_precision(x, 8, 7)
    return high.astype(bf16), (x - high).astype(bf16)


def dot_split(a, b, dims=(((1,), (0,)), ((), ()))):
    return dot(a, b[0], dims) + dot(a, b[1], dims)


def body(resid, heads, down_matrix, up, scale, value_matrix, target):
    share = target.shape[0]
    tp = resid.shape[0] // share
    tokens = resid.shape[0] * lax.axis_size(ROWS)
    loss_scale = 1.0 / tokens**0.5
    gain = scale.astype(f32)
    rank = up.shape[0]
    width = target.shape[1]

    up_high, up_low = split(up.astype(f32) * gain)
    weights = jnp.concatenate(
        [
            dot(up_high, value_matrix) + dot(up_low, value_matrix),
            dot(up, up, NT),
            jnp.zeros((rank, rank), f32),
        ],
        axis=1,
    )
    columns = weights.shape[1]

    wide = resid.astype(f32)
    part = jnp.concatenate(
        [
            dot((wide * gain).astype(bf16), value_matrix),
            dot(heads, down_matrix),
            dot(resid, up, NT),
        ],
        axis=1,
    )
    squares = jnp.sum(wide * wide, axis=1).reshape(tp, 1, share)
    tail = jnp.concatenate(split(squares), axis=1)
    tail = jnp.pad(tail, ((0, 0), (0, 14), (0, columns - share)))
    pieces = jnp.concatenate(
        [
            part.astype(bf16).reshape(tp, share, columns),
            jnp.broadcast_to(weights.astype(bf16), (tp, rank, columns)),
            tail,
        ],
        axis=1,
    )
    pieces = lax.all_to_all(pieces, TP, 0, 0, tiled=True)
    total = jnp.sum(pieces.astype(f32), axis=0)
    through = split(total[share : share + rank, :width])
    gram = split(total[share : share + rank, width : width + rank])
    square_sums = total[share + rank, :share] + total[share + rank + 1, :share]

    down_b = total[:share, width : width + rank].astype(bf16)
    down_wide = down_b.astype(f32)
    along = total[:share, width + rank :]
    hidden_up = along + 0.5 * dot_split(down_b, gram)
    square_sums = square_sums + 0.5 * jnp.sum(down_wide * (along + hidden_up), axis=1)
    inverse_rms = lax.rsqrt(square_sums / MODEL_WIDTH + EPSILON)[:, None]
    sums = inverse_rms * (total[:share, :width] + 0.5 * dot_split(down_b, through))
    error = (sums - target.astype(f32)) * loss_scale
    inner = jnp.sum(error * sums, axis=1, keepdims=True) / MODEL_WIDTH
    high, low = split(error)
    down_grad = dot_split(high, through, NT) + dot(low, through[0], NT)
    down_grad = 0.5 * inverse_rms * (down_grad - inner * inverse_rms * hidden_up)
    sent = jnp.concatenate(
        [
            error * inverse_rms,
            down_wide,
            down_grad,
            down_wide * (inner * inverse_rms * inverse_rms),
        ],
        axis=1,
    ).astype(bf16)
    every = lax.all_to_all(jnp.broadcast_to(sent, (tp, *sent.shape)), TP, 0, 0, tiled=True)
    every = every.reshape(tp * share, -1)

    error_all = every[:, :width]
    down_all = every[:, width : width + rank]
    grad_all = every[:, width + rank : width + 2 * rank]
    weighted_all = every[:, width + 2 * rank :]
    hidden = (wide + 0.5 * dot(down_all, up)).astype(bf16)
    value_part = dot(hidden, error_all, TN)
    a_part = dot(heads, grad_all, TN)
    cross = split(dot(error_all, down_all, TN))
    b_part = 0.5 * (gain[:, None] * dot_split(value_matrix, cross) - dot(hidden, weighted_all, TN))
    gain_part = jnp.sum(value_part * value_matrix.astype(f32), axis=1)

    blocks = [lax.axis_size(a) for a in ROWS]
    own = value_part.shape[0] // (blocks[0] * blocks[1] * blocks[2])
    small = jnp.concatenate([a_part, b_part], axis=1).reshape(*blocks, own, 2 * rank)
    gain_part = jnp.pad(
        gain_part.reshape(*blocks, 1, own), ((0, 0),) * 3 + ((0, 7), (0, 2 * rank - own))
    )
    small = row_sum(jnp.concatenate([small, gain_part], axis=3))
    value_part = row_sum(value_part.reshape(*blocks, own, width))
    first = lax.axis_index(ROWS) * own
    own_gain = lax.dynamic_slice_in_dim(gain, first, own, 0)
    value_grad = (value_part * own_gain[:, None]).astype(bf16)

    small = pair_gather(small.astype(bf16), "y_hi")
    small = lax.all_to_all(
        jnp.broadcast_to(small, (blocks[1], *small.shape)), "z", 0, 0, tiled=True
    )
    small = pair_gather(small, "core")
    small = small.transpose(2, 1, 0, 3, 4)
    a_b = small[:, :, :, :own].reshape(-1, 2 * rank).astype(f32)
    gain_grad = small[:, :, :, own, :own].reshape(-1).astype(f32)
    return (sums.astype(bf16), value_grad, a_b[:, :rank], a_b[:, rank:].T, gain_grad)


def row_sum(part):
    part = pair_sum(part, "core", 2)
    part = pair_sum(part, "y_hi", 0)
    part = lax.all_to_all(part.astype(bf16), "z", 0, 0, tiled=True)
    return jnp.sum(part.astype(f32), axis=0)


def swap(x, axis):
    return lax.ppermute(x, axis, [(0, 1), (1, 0)])


def pair_sum(x, axis, dim):
    me = lax.axis_index(axis)
    mine = lax.dynamic_index_in_dim(x, me, dim, keepdims=False)
    other = lax.dynamic_index_in_dim(x, 1 - me, dim, keepdims=False)
    return mine.astype(f32) + swap(other.astype(bf16), axis).astype(f32)


def pair_gather(x, axis):
    me = lax.axis_index(axis)
    other = swap(x, axis)
    first = me == 0
    return jnp.stack([jnp.where(first, x, other), jnp.where(first, other, x)])


def solution(mesh):
    rows, tp = mesh.shape["rows"], mesh.shape["tp"]
    y_hi, core, y_lo = 2, 2, 2
    fine = Mesh(
        mesh.devices.reshape(y_hi, rows // (y_hi * core), core, tp // y_lo, y_lo), (*ROWS, *TP)
    )
    in_specs = (
        P(ROWS, TP),
        P(ROWS, TP),
        P(TP, None),
        P(None, TP),
        P(TP),
        P(TP, None),
        P((*ROWS, *TP), None),
    )
    out_specs = (
        P((*ROWS, *TP), None),
        P((*TP, *ROWS), None),
        P(TP, None),
        P(None, TP),
        P(TP),
    )
    return jax.shard_map(body, mesh=fine, in_specs=in_specs, out_specs=out_specs, check_vma=False)
```

```python
import functools

import jax
import jax.numpy as jnp
from jax import lax
from jax.experimental import pallas as pl
from jax.experimental.pallas import tpu as pltpu
from jax.sharding import Mesh, PartitionSpec as P

MODEL_WIDTH = 8192
EPSILON = 1e-06
TP = ("x", "y_lo")
ROWS = ("y_hi", "z", "core")
bf16 = jnp.bfloat16
f32 = jnp.float32
NN = (((1,), (0,)), ((), ()))
NT = (((1,), (1,)), ((), ()))
TN = (((0,), (0,)), ((), ()))
VMEM_LIMIT = 48 * 2**20


def dot(a, b, dims=NN):
    return lax.dot_general(a, b, dims, preferred_element_type=f32)


def split(x):
    high = lax.reduce_precision(x, 8, 7)
    return high.astype(bf16), (x - high).astype(bf16)


def dot_split(a, b, dims=NN):
    return dot(a, b[0], dims) + dot(a, b[1], dims)


def halves(x):
    high = x.astype(bf16)
    return high, (x - high.astype(f32)).astype(bf16)


def weights_kernel(half_ref, up_ref, gain_ref, matrix_ref, out_ref):
    half = half_ref[...]
    high, low = halves(half.astype(f32) * gain_ref[...])
    width = matrix_ref.shape[1]
    out_ref[:, :width] = dot(high, matrix_ref[...]) + dot(low, matrix_ref[...])
    gram = dot(half, up_ref[...], NT)
    out_ref[:, width:] = jnp.concatenate([gram, jnp.zeros_like(gram)], axis=1)


def weight_products(half, up, gain, matrix):
    columns = matrix.shape[1] + 2 * up.shape[0]
    return pl.pallas_call(
        weights_kernel,
        out_shape=jax.ShapeDtypeStruct((half.shape[0], columns), f32),
        compiler_params=pltpu.CompilerParams(vmem_limit_bytes=VMEM_LIMIT),
        cost_estimate=pl.CostEstimate(
            flops=4 * half.size * matrix.shape[1], bytes_accessed=2 * matrix.size, transcendentals=0
        ),
    )(half, up, gain, matrix)


def project_kernel(share, resid_ref, heads_ref, gain_ref, matrix_ref, down_ref, up_ref, out_ref):
    width = matrix_ref.shape[1]
    resid = resid_ref[...]
    wide = resid.astype(f32)
    values = dot((wide * gain_ref[...]).astype(bf16), matrix_ref[...])
    small = dot(heads_ref[...], down_ref[...]) + dot(resid, up_ref[...])
    high, low = halves(wide * wide)
    ones = jnp.ones((16, wide.shape[1]), bf16)
    line = lax.broadcasted_iota(jnp.int32, (16, share), 0)
    for piece in range(out_ref.shape[0]):
        rows = slice(piece * share, (piece + 1) * share)
        out_ref[piece, :share, :width] = values[rows].astype(bf16)
        out_ref[piece, :share, width:] = small[rows].astype(bf16)
        squares = dot(ones, high[rows], NT) + dot(ones, low[rows], NT)
        first = squares.astype(bf16).astype(f32)
        tail = jnp.where(line == 0, first, jnp.where(line == 1, squares - first, 0.0))
        out_ref[piece, share:, :] = jnp.zeros((16, out_ref.shape[2]), bf16)
        out_ref[piece, share:, :share] = tail.astype(bf16)


def project(resid, heads, gain, matrix, down, up, share):
    tokens, features = resid.shape
    width = matrix.shape[1]
    pieces, group = tokens // share, 2
    rows = group * share
    whole = lambda i: (0, 0)
    return pl.pallas_call(
        functools.partial(project_kernel, share),
        grid=(pieces // group,),
        in_specs=[
            pl.BlockSpec((rows, features), lambda i: (i, 0)),
            pl.BlockSpec((rows, features), lambda i: (i, 0)),
            pl.BlockSpec((1, features), whole),
            pl.BlockSpec((features, width), whole),
            pl.BlockSpec(down.shape, whole),
            pl.BlockSpec(up.shape, whole),
        ],
        out_specs=pl.BlockSpec((group, share + 16, width + 128), lambda i: (i, 0, 0)),
        out_shape=jax.ShapeDtypeStruct((pieces, share + 16, width + 128), bf16),
        compiler_params=pltpu.CompilerParams(vmem_limit_bytes=VMEM_LIMIT),
        cost_estimate=pl.CostEstimate(
            flops=2 * tokens * features * (width + 256),
            bytes_accessed=4 * tokens * features + 2 * features * width,
            transcendentals=0,
        ),
    )(resid, heads, gain, matrix, down, up)


def gradients_kernel(
    core_ref, every_ref, resid_ref, heads_ref, up_ref, gain_ref, matrix_ref,
    value_ref, value_sent_ref, small_ref, small_sent_ref, cross_ref,
):
    width = matrix_ref.shape[1]
    rank = up_ref.shape[0]
    error = every_ref[:, :width]
    down = every_ref[:, width : width + rank]

    @pl.when(pl.program_id(0) == 0)
    def _():
        high, low = halves(dot(error, down, TN))
        cross_ref[0] = high
        cross_ref[1] = low

    core = core_ref[0]
    matrix = matrix_ref[...]
    hidden = (resid_ref[...].astype(f32) + 0.5 * dot(down, up_ref[...])).astype(bf16)
    value = dot(hidden, error, TN)
    a_part = dot(heads_ref[...], every_ref[:, width + rank : width + 2 * rank], TN)
    b_part = dot(hidden, every_ref[:, width + 2 * rank :], TN)
    crossed = dot(matrix, cross_ref[0]) + dot(matrix, cross_ref[1])
    b_part = 0.5 * (gain_ref[...] * crossed - b_part)
    small = jnp.concatenate([a_part, b_part], axis=1)
    gain_part = jnp.sum(value * matrix.astype(f32), axis=1, keepdims=True)
    pieces, own = 2 * value_ref.shape[0], value_ref.shape[1]
    lane = lax.broadcasted_iota(jnp.int32, small.shape, 1)
    line = lax.rem(lax.broadcasted_iota(jnp.int32, small.shape, 0), own)
    spread = jnp.where(lane == line, gain_part, 0.0).reshape(pieces, own, -1)
    gain_row = jnp.sum(spread, axis=1, keepdims=True)
    row = lax.broadcasted_iota(jnp.int32, (pieces // 2, 16, small.shape[1]), 1)

    value = value.reshape(pieces // 2, 2, own, width)
    small = small.reshape(pieces // 2, 2, own, -1)
    gain_row = gain_row.reshape(pieces // 2, 2, 1, -1)
    first = core == 0
    value_ref[...] = jnp.where(first, value[:, 0], value[:, 1]).astype(bf16)
    value_sent_ref[...] = jnp.where(first, value[:, 1], value[:, 0]).astype(bf16)
    small_ref[:, :own] = jnp.where(first, small[:, 0], small[:, 1])
    small_sent_ref[:, :own] = jnp.where(first, small[:, 1], small[:, 0]).astype(bf16)
    kept = jnp.where(first, gain_row[:, 0], gain_row[:, 1])
    sent = jnp.where(first, gain_row[:, 1], gain_row[:, 0])
    small_ref[:, own:] = jnp.where(row == 0, kept, 0.0)
    small_sent_ref[:, own:] = jnp.where(row == 0, sent, 0.0).astype(bf16)


def gradients(core, every, resid, heads, up, gain, matrix, own):
    tokens, features = resid.shape
    width, rank = matrix.shape[1], up.shape[0]
    block = 256
    pieces, group = features // (2 * own), block // (2 * own)
    value = jax.ShapeDtypeStruct((pieces, own, width), bf16)
    small = jax.ShapeDtypeStruct((pieces, own + 16, 2 * rank), f32)
    small_sent = jax.ShapeDtypeStruct((pieces, own + 16, 2 * rank), bf16)
    return pl.pallas_call(
        gradients_kernel,
        grid=(features // block,),
        in_specs=[
            pl.BlockSpec(memory_space=pltpu.SMEM),
            pl.BlockSpec(every.shape, lambda i: (0, 0)),
            pl.BlockSpec((tokens, block), lambda i: (0, i)),
            pl.BlockSpec((tokens, block), lambda i: (0, i)),
            pl.BlockSpec((rank, block), lambda i: (0, i)),
            pl.BlockSpec((block, 1), lambda i: (i, 0)),
            pl.BlockSpec((block, width), lambda i: (i, 0)),
        ],
        out_specs=[
            pl.BlockSpec((group, own, width), lambda i: (i, 0, 0)),
            pl.BlockSpec((group, own, width), lambda i: (i, 0, 0)),
            pl.BlockSpec((group, own + 16, 2 * rank), lambda i: (i, 0, 0)),
            pl.BlockSpec((group, own + 16, 2 * rank), lambda i: (i, 0, 0)),
        ],
        out_shape=[value, value, small, small_sent],
        scratch_shapes=[pltpu.VMEM((2, width, rank), bf16)],
        compiler_params=pltpu.CompilerParams(vmem_limit_bytes=VMEM_LIMIT),
        cost_estimate=pl.CostEstimate(
            flops=2 * tokens * features * (width + 4 * rank),
            bytes_accessed=4 * tokens * features + 8 * features * width,
            transcendentals=0,
        ),
    )(core, every, resid, heads, up, gain, matrix)


def body(resid, heads, down_matrix, up, scale, value_matrix, target):
    share, width = target.shape
    tp = resid.shape[0] // share
    tokens = resid.shape[0] * lax.axis_size(ROWS)
    loss_scale = 1.0 / tokens**0.5
    rank, features = up.shape
    core = lax.axis_index("core")
    gain = scale.astype(f32)

    half = lax.dynamic_slice_in_dim(up, core * (rank // 2), rank // 2, 0)
    weights = weight_products(half, up, gain[None, :], value_matrix)
    weights = weights + swap(weights, "y_lo")

    pieces = project(
        resid,
        heads,
        gain[None, :],
        value_matrix,
        jnp.pad(down_matrix, ((0, 0), (0, rank))),
        jnp.pad(up.T, ((0, 0), (rank, 0))),
        share,
    )
    pieces = lax.all_to_all(pieces, TP, 0, 0, tiled=True)
    for distance in (1, 2):
        weights = weights + swap(weights, "x", distance)
    weights = pair_gather(weights, "core").reshape(rank, -1)
    through = split(weights[:, :width])
    gram = split(weights[:, width : width + rank])
    total = jnp.sum(pieces.astype(f32), axis=0)
    square_sums = total[share, :share] + total[share + 1, :share]

    down_b = total[:share, width : width + rank].astype(bf16)
    down_wide = down_b.astype(f32)
    along = total[:share, width + rank :]
    hidden_up = along + 0.5 * dot_split(down_b, gram)
    square_sums = square_sums + 0.5 * jnp.sum(down_wide * (along + hidden_up), axis=1)
    inverse_rms = lax.rsqrt(square_sums / MODEL_WIDTH + EPSILON)[:, None]
    sums = inverse_rms * (total[:share, :width] + 0.5 * dot_split(down_b, through))
    error = (sums - target.astype(f32)) * loss_scale
    inner = jnp.sum(error * sums, axis=1, keepdims=True) / MODEL_WIDTH
    high, low = split(error)
    down_grad = dot_split(high, through, NT) + dot(low, through[0], NT)
    down_grad = 0.5 * inverse_rms * (down_grad - inner * inverse_rms * hidden_up)
    sent = jnp.concatenate(
        [
            error * inverse_rms,
            down_wide,
            down_grad,
            down_wide * (inner * inverse_rms * inverse_rms),
        ],
        axis=1,
    ).astype(bf16)
    every = lax.all_to_all(jnp.broadcast_to(sent, (tp, *sent.shape)), TP, 0, 0, tiled=True)
    every = every.reshape(tp * share, -1)

    y_size, z_size, core_size = (lax.axis_size(a) for a in ROWS)
    own = features // (y_size * z_size * core_size)
    value, value_sent, small, small_sent = gradients(
        core.reshape(1), every, resid, heads, up, gain[:, None], value_matrix, own
    )

    rows = own + 8
    small_got = swap(small_sent, "core")
    value_got = swap(value_sent, "core")
    small = (small[:, :rows] + small_got[:, :rows].astype(f32)).astype(bf16)
    small = small.reshape(y_size, z_size, rows, -1).transpose(1, 0, 2, 3)
    small, value, value_got = lax.optimization_barrier((small, value, value_got))
    small = lax.all_to_all(small, "z", 0, 0, tiled=True)

    me = lax.axis_index("y_hi")
    value = value.reshape(y_size, z_size, own, width)
    value_got = value_got.reshape(y_size, z_size, own, width)
    pick = lambda x, i: lax.dynamic_index_in_dim(x, i, 0, keepdims=False).astype(f32)
    other = swap((pick(value, 1 - me) + pick(value_got, 1 - me)).astype(bf16), "y_hi")
    value = (pick(value, me) + pick(value_got, me) + other.astype(f32)).astype(bf16)
    small, value = lax.optimization_barrier((small, value))
    small = jnp.sum(small.astype(f32), axis=0)
    small = (small + swap(small, "y_hi")).astype(bf16)

    small = jnp.broadcast_to(small.reshape(1, own, -1), (z_size, own, y_size * rows * 2 * rank // own))
    value = lax.all_to_all(jnp.concatenate([value, small], axis=2), "z", 0, 0, tiled=True)
    small = pair_gather(value[:, :, width:], "core")
    small = small.reshape(core_size, z_size, y_size, rows, 2 * rank).transpose(2, 1, 0, 3, 4)
    a_b = small[:, :, :, :own].reshape(-1, 2 * rank).astype(f32)
    gain_grad = small[:, :, :, own, :own].reshape(-1).astype(f32)

    value = jnp.sum(value[:, :, :width].astype(f32), axis=0)
    own_gain = lax.dynamic_slice_in_dim(gain, lax.axis_index(ROWS) * own, own, 0)
    value_grad = (value * own_gain[:, None]).astype(bf16)
    return (sums.astype(bf16), value_grad, a_b[:, :rank], a_b[:, rank:].T, gain_grad)


def swap(x, axis, distance=1):
    return lax.ppermute(x, axis, [(i, i ^ distance) for i in range(lax.axis_size(axis))])


def pair_gather(x, axis):
    me = lax.axis_index(axis)
    other = swap(x, axis)
    first = me == 0
    return jnp.stack([jnp.where(first, x, other), jnp.where(first, other, x)])


def solution(mesh):
    rows, tp = mesh.shape["rows"], mesh.shape["tp"]
    y_hi, core, y_lo = 2, 2, 2
    fine = Mesh(
        mesh.devices.reshape(y_hi, rows // (y_hi * core), core, tp // y_lo, y_lo), (*ROWS, *TP)
    )
    in_specs = (
        P(ROWS, TP),
        P(ROWS, TP),
        P(TP, None),
        P(None, TP),
        P(TP),
        P(TP, None),
        P((*ROWS, *TP), None),
    )
    out_specs = (
        P((*ROWS, *TP), None),
        P((*TP, *ROWS), None),
        P(TP, None),
        P(None, TP),
        P(TP),
    )
    return jax.shard_map(body, mesh=fine, in_specs=in_specs, out_specs=out_specs, check_vma=False)
```

```python
import functools

import jax
import jax.numpy as jnp
from jax import lax
from jax.experimental import pallas as pl
from jax.experimental.pallas import tpu as pltpu
from jax.sharding import Mesh, PartitionSpec as P

MODEL_WIDTH = 8192
EPSILON = 1e-06
TP = ("x", "y_lo")
ROWS = ("y_hi", "z", "core")
bf16 = jnp.bfloat16
f32 = jnp.float32
NN = (((1,), (0,)), ((), ()))
NT = (((1,), (1,)), ((), ()))
TN = (((0,), (0,)), ((), ()))
LANES = 128
VMEM_LIMIT = 48 * 2**20
VMEM_WHOLE = 60 * 2**20


def dot(a, b, dims=NN):
    return lax.dot_general(a, b, dims, preferred_element_type=f32)


def split(x):
    high = x.astype(bf16)
    return high, (x - high.astype(f32)).astype(bf16)


def dot_split(a, b, dims=NN):
    return dot(a, b[0], dims) + dot(a, b[1], dims)


def project_kernel(
    share, resid_ref, heads_ref, gain_ref, matrix_ref, down_ref, up_ref, out_ref, weights_ref
):
    rank, width = up_ref.shape[0], matrix_ref.shape[1]
    gain = gain_ref[...].astype(f32)

    @pl.when(pl.program_id(0) == 0)
    def _():
        high, low = split(up_ref[...].astype(f32) * gain)
        weights_ref[:, :width] = dot(high, matrix_ref[...]) + dot(low, matrix_ref[...])
        gram = dot(up_ref[...], up_ref[...], NT)
        weights_ref[:, width:] = jnp.concatenate([gram, jnp.zeros_like(gram)], axis=1)

    resid = resid_ref[...]
    wide = resid.astype(f32)
    values = dot((wide * gain).astype(bf16), matrix_ref[...])
    small = [dot(heads_ref[...], down_ref[...], NT), dot(resid, up_ref[...], NT)]
    small = jnp.concatenate(small, axis=1)
    high, low = split(wide * wide)
    ones = jnp.ones((rank, wide.shape[1]), bf16)
    line = lax.broadcasted_iota(jnp.int32, (rank, share // 2), 0)
    for piece in range(out_ref.shape[0]):
        rows = slice(piece * share, (piece + 1) * share)
        out_ref[piece, :share, :width] = values[rows].astype(bf16)
        out_ref[piece, :share, width:] = small[rows].astype(bf16)
        lines = jnp.zeros(line.shape, f32)
        for part in range(2):
            rows = slice(piece * share + part * (share // 2), piece * share + (part + 1) * (share // 2))
            squares = dot(ones, high[rows], NT) + dot(ones, low[rows], NT)
            first = squares.astype(bf16).astype(f32)
            lines = jnp.where(line == part, first, lines)
            lines = jnp.where(line == 2 + part, squares - first, lines)
        blank = [jnp.zeros((rank, rank), f32), lines, jnp.zeros((rank, rank - share // 2), f32)]
        out_ref[piece, share:, :width] = weights_ref[:, :width].astype(bf16)
        tail = weights_ref[:, width:] + jnp.concatenate(blank, axis=1)
        out_ref[piece, share:, width:] = tail.astype(bf16)


def project(resid, heads, gain, matrix, down, up, share):
    tokens, features = resid.shape
    rank, width = up.shape[0], matrix.shape[1]
    pieces, group = tokens // share, 2
    rows, columns = group * share, width + 2 * rank
    whole = lambda i: (0, 0)
    return pl.pallas_call(
        functools.partial(project_kernel, share),
        grid=(pieces // group,),
        in_specs=[
            pl.BlockSpec((rows, features), lambda i: (i, 0)),
            pl.BlockSpec((rows, features), lambda i: (i, 0)),
            pl.BlockSpec((1, features), whole),
            pl.BlockSpec((features, width), whole),
            pl.BlockSpec(down.shape, whole),
            pl.BlockSpec(up.shape, whole),
        ],
        out_specs=pl.BlockSpec((group, share + rank, columns), lambda i: (i, 0, 0)),
        out_shape=jax.ShapeDtypeStruct((pieces, share + rank, columns), bf16),
        scratch_shapes=[pltpu.VMEM((rank, columns), f32)],
        compiler_params=pltpu.CompilerParams(vmem_limit_bytes=VMEM_WHOLE),
        cost_estimate=pl.CostEstimate(
            flops=2 * tokens * features * (width + 256),
            bytes_accessed=4 * tokens * features + 2 * features * width,
            transcendentals=0,
        ),
    )(resid, heads, gain, matrix, down, up)


def owner_kernel(loss_scale, pieces_ref, target_ref, values_ref, every_ref, sent_ref, sems):
    share, width = target_ref.shape
    tp = pieces_ref.shape[0]
    rank = pieces_ref.shape[1] - share
    total = functools.reduce(jnp.add, [pieces_ref[i].astype(f32) for i in range(tp)])
    through = split(total[share:, :width])
    gram = split(total[share:, width : width + rank])
    lines = total[share : share + 8, width + rank : width + rank + share // 2]
    lines = lines[0:2] + lines[2:4]
    diagonal = (share // 2, share // 2)
    diagonal = lax.broadcasted_iota(jnp.int32, diagonal, 0) == lax.broadcasted_iota(jnp.int32, diagonal, 1)
    squares = jnp.concatenate(
        [
            jnp.sum(jnp.where(diagonal, lines[i : i + 1], 0.0), axis=1, keepdims=True)
            for i in range(2)
        ],
        axis=0,
    )

    down_b = total[:share, width : width + rank].astype(bf16)
    down_wide = down_b.astype(f32)
    along = total[:share, width + rank :]
    hidden_up = along + 0.5 * dot_split(down_b, gram)
    squares = squares + 0.5 * jnp.sum(down_wide * (along + hidden_up), axis=1, keepdims=True)
    inverse_rms = lax.rsqrt(squares / MODEL_WIDTH + EPSILON)
    sums = inverse_rms * (total[:share, :width] + 0.5 * dot_split(down_b, through))
    values_ref[...] = sums.astype(bf16)
    error = (sums - target_ref[...].astype(f32)) * loss_scale
    inner = jnp.sum(error * sums, axis=1, keepdims=True) / MODEL_WIDTH
    high, low = split(error)
    down_grad = dot_split(high, through, NT) + dot(low, through[0], NT)
    down_grad = 0.5 * inverse_rms * (down_grad - inner * inverse_rms * hidden_up)
    weighted = down_wide * (inner * inverse_rms * inverse_rms)
    sent_ref[:, :width] = (error * inverse_rms).astype(bf16)
    sent_ref[:, width : width + 2 * rank] = jnp.concatenate([down_wide, down_grad], axis=1).astype(bf16)
    sent_ref[:, width + 2 * rank :] = weighted.astype(bf16)
    copies = [pltpu.make_async_copy(sent_ref, every_ref.at[i], sems.at[i]) for i in range(tp)]
    for copy in copies:
        copy.start()
    for copy in copies:
        copy.wait()


def owner(pieces, target, loss_scale):
    share, width = target.shape
    tp, rank = pieces.shape[0], pieces.shape[1] - share
    sent = (share, width + 3 * rank)
    vmem = pl.BlockSpec(memory_space=pltpu.VMEM)
    return pl.pallas_call(
        functools.partial(owner_kernel, loss_scale),
        in_specs=[vmem, vmem],
        out_specs=[vmem, pl.BlockSpec(memory_space=pl.ANY)],
        out_shape=[
            jax.ShapeDtypeStruct((share, width), bf16),
            jax.ShapeDtypeStruct((tp, *sent), bf16),
        ],
        scratch_shapes=[pltpu.VMEM(sent, bf16), pltpu.SemaphoreType.DMA((tp,))],
        compiler_params=pltpu.CompilerParams(vmem_limit_bytes=VMEM_LIMIT),
    )(pieces, target)


def gradients_kernel(
    core_ref, every_ref, resid_ref, heads_ref, up_ref, gain_ref, matrix_ref,
    kept_ref, small_ref, sent_ref, cross_ref,
):
    width = matrix_ref.shape[1]
    rank = up_ref.shape[0]
    error = every_ref[:, :width]
    down = every_ref[:, width : width + rank]

    @pl.when(pl.program_id(0) == 0)
    def _():
        high, low = split(dot(error, down, TN))
        cross_ref[0] = high
        cross_ref[1] = low

    core = core_ref[0]
    matrix = matrix_ref[...]
    hidden = (resid_ref[...].astype(f32) + 0.5 * dot(down, up_ref[...])).astype(bf16)
    value = dot(hidden, error, TN)
    a_part = dot(heads_ref[...], every_ref[:, width + rank : width + 2 * rank], TN)
    b_part = dot(hidden, every_ref[:, width + 2 * rank :], TN)
    crossed = dot(matrix, cross_ref[0]) + dot(matrix, cross_ref[1])
    b_part = 0.5 * (gain_ref[...] * crossed - b_part)
    small = jnp.concatenate([a_part, b_part], axis=1)
    gain_part = jnp.sum(value * matrix.astype(f32), axis=1, keepdims=True)
    group, own = kept_ref.shape[:2]
    lane = lax.broadcasted_iota(jnp.int32, small.shape, 1)
    line = lax.rem(lax.broadcasted_iota(jnp.int32, small.shape, 0), LANES)
    spread = jnp.where(lane == line, gain_part, 0.0).reshape(2 * group, own, LANES)
    gain_line = jnp.sum(spread, axis=1, keepdims=True)
    row = lax.broadcasted_iota(jnp.int32, (2 * group, own, LANES), 1)
    gain_line = jnp.where(row == 0, gain_line, 0.0)
    small = jnp.concatenate([small.reshape(2 * group, own, -1), gain_line], axis=2)
    small = small.reshape(group, 2, own, -1)
    value = value.reshape(group, 2, own, width)
    first = core == 0
    kept_ref[...] = jnp.where(first, value[:, 0], value[:, 1]).astype(bf16)
    small_ref[...] = jnp.where(first, small[:, 0], small[:, 1])
    sent_ref[:, :, :width] = jnp.where(first, value[:, 1], value[:, 0]).astype(bf16)
    sent_ref[:, :, width:] = jnp.where(first, small[:, 1], small[:, 0]).astype(bf16)


def gradients(core, every, resid, heads, up, gain, matrix, own):
    tokens, features = resid.shape
    width, rank = matrix.shape[1], up.shape[0]
    block = 256
    pieces, group = features // (2 * own), block // (2 * own)
    shapes = [
        jax.ShapeDtypeStruct((pieces, own, width), bf16),
        jax.ShapeDtypeStruct((pieces, own, 2 * rank + LANES), f32),
        jax.ShapeDtypeStruct((pieces, own, width + 2 * rank + LANES), bf16),
    ]
    return pl.pallas_call(
        gradients_kernel,
        grid=(features // block,),
        in_specs=[
            pl.BlockSpec(memory_space=pltpu.SMEM),
            pl.BlockSpec(every.shape, lambda i: (0, 0)),
            pl.BlockSpec((tokens, block), lambda i: (0, i)),
            pl.BlockSpec((tokens, block), lambda i: (0, i)),
            pl.BlockSpec((rank, block), lambda i: (0, i)),
            pl.BlockSpec((block, 1), lambda i: (i, 0)),
            pl.BlockSpec((block, width), lambda i: (i, 0)),
        ],
        out_specs=[pl.BlockSpec((group, *s.shape[1:]), lambda i: (i, 0, 0)) for s in shapes],
        out_shape=shapes,
        scratch_shapes=[pltpu.VMEM((2, width, rank), bf16)],
        compiler_params=pltpu.CompilerParams(vmem_limit_bytes=VMEM_LIMIT),
        cost_estimate=pl.CostEstimate(
            flops=2 * tokens * features * (width + 4 * rank),
            bytes_accessed=4 * tokens * features + 8 * features * width,
            transcendentals=0,
        ),
    )(core, every, resid, heads, up, gain, matrix)


def assemble_kernel(core_ref, mine_ref, got_ref, a_ref, b_ref, gain_ref):
    z_size, own = mine_ref.shape[:2]
    rank, features = a_ref.shape
    together = LANES // (2 * own)
    first = core_ref[0] == 0
    for y in range(2):
        for start in range(0, z_size, together):
            lines, gain_line = [], jnp.zeros((1, LANES), f32)
            for z in range(start, start + together):
                mine = mine_ref[z].astype(f32)
                got = got_ref[z].astype(f32)
                lanes = slice(y * LANES, (y + 1) * LANES)
                lines += [
                    jnp.where(first, mine[:, lanes], got[:, lanes]),
                    jnp.where(first, got[:, lanes], mine[:, lanes]),
                ]
                gain_line += (mine + got)[y * 8 : y * 8 + 1, 2 * LANES :]
            both = jnp.concatenate(lines, axis=0).T
            place = y * (features // 2) + start * 2 * own
            a_ref[:, place : place + LANES] = both[:rank]
            b_ref[:, place : place + LANES] = both[rank:]
            gain_ref[:, place : place + LANES] = gain_line


def assemble(core, mine, got, rank):
    z_size, own = mine.shape[:2]
    features = 2 * z_size * 2 * own
    whole = jax.ShapeDtypeStruct((rank, features), f32)
    vmem = pl.BlockSpec(memory_space=pltpu.VMEM)
    return pl.pallas_call(
        assemble_kernel,
        in_specs=[pl.BlockSpec(memory_space=pltpu.SMEM), vmem, vmem],
        out_specs=[vmem, vmem, vmem],
        out_shape=[whole, whole, jax.ShapeDtypeStruct((1, features), f32)],
        compiler_params=pltpu.CompilerParams(vmem_limit_bytes=VMEM_LIMIT),
    )(core, mine, got)


def body(resid, heads, down_matrix, up, scale, value_matrix, target):
    share, width = target.shape
    tp = resid.shape[0] // share
    tokens = resid.shape[0] * lax.axis_size(ROWS)
    rank, features = up.shape
    core = lax.axis_index("core")
    gain = scale.astype(f32)

    pieces = project(resid, heads, scale.reshape(1, -1), value_matrix, down_matrix.T, up, share)
    pieces = lax.all_to_all(pieces, TP, 0, 0, tiled=True)
    values, every = owner(pieces, target, 1.0 / tokens**0.5)
    every = lax.all_to_all(every, TP, 0, 0, tiled=True)
    every = every.reshape(tp * share, -1)

    y_size, z_size, core_size = (lax.axis_size(a) for a in ROWS)
    own = features // (y_size * z_size * core_size)
    kept, small, sent = gradients(
        core.reshape(1), every, resid, heads, up, gain[:, None], value_matrix, own
    )

    got = swap(sent, "core")
    small = small + got[:, :, width:].astype(f32)
    small = jnp.concatenate([small[:, :, : 2 * rank], small[:, :8, 2 * rank :]], axis=1)
    small = small.astype(bf16).reshape(y_size, z_size, own + 8, -1).transpose(1, 0, 2, 3)
    small = lax.all_to_all(small, "z", 0, 0, tiled=True)

    me = lax.axis_index("y_hi")
    kept = kept.reshape(y_size, z_size, own, width)
    got = got.reshape(y_size, z_size, own, -1)[..., :width]
    pick = lambda x, i: lax.dynamic_index_in_dim(x, i, 0, keepdims=False).astype(f32)
    other = swap((pick(kept, 1 - me) + pick(got, 1 - me)).astype(bf16), "y_hi")
    value = (pick(kept, me) + pick(got, me) + other.astype(f32)).astype(bf16)

    small = jnp.sum(small.astype(f32), axis=0)
    small = (small + swap(small, "y_hi")).astype(bf16)

    gains = small[:, own:].reshape(-1, small.shape[-1])
    small = jnp.concatenate([*small[:, :own], gains], axis=1)
    small = jnp.broadcast_to(small, (z_size, *small.shape))
    value = lax.all_to_all(jnp.concatenate([value, small], axis=2), "z", 0, 0, tiled=True)
    small = value[:, :, width:]
    a_grad, b_grad, gain_grad = assemble(core.reshape(1), small, swap(small, "core"), rank)

    value = jnp.sum(value[:, :, :width].astype(f32), axis=0)
    own_gain = lax.dynamic_slice_in_dim(gain, lax.axis_index(ROWS) * own, own, 0)
    value_grad = (value * own_gain[:, None]).astype(bf16)
    return (values, value_grad, a_grad.T, b_grad, gain_grad.reshape(-1))


def swap(x, axis):
    return lax.ppermute(x, axis, [(0, 1), (1, 0)])


def solution(mesh):
    rows, tp = mesh.shape["rows"], mesh.shape["tp"]
    y_hi, core, y_lo = 2, 2, 2
    fine = Mesh(
        mesh.devices.reshape(y_hi, rows // (y_hi * core), core, tp // y_lo, y_lo), (*ROWS, *TP)
    )
    in_specs = (
        P(ROWS, TP),
        P(ROWS, TP),
        P(TP, None),
        P(None, TP),
        P(TP),
        P(TP, None),
        P((*ROWS, *TP), None),
    )
    out_specs = (
        P((*ROWS, *TP), None),
        P((*TP, *ROWS), None),
        P(TP, None),
        P(None, TP),
        P(TP),
    )
    return jax.shard_map(body, mesh=fine, in_specs=in_specs, out_specs=out_specs, check_vma=False)
```

```python
import functools

import jax
import jax.numpy as jnp
from jax import lax
from jax.experimental import pallas as pl
from jax.experimental.pallas import tpu as pltpu
from jax.sharding import Mesh, PartitionSpec as P

MODEL_WIDTH = 8192
EPSILON = 1e-06
TP = ("x", "y_lo")
Z = ("z_pair", "z_odd")
ROWS = ("y_hi", *Z, "core")
bf16 = jnp.bfloat16
f32 = jnp.float32
NN = (((1,), (0,)), ((), ()))
NT = (((1,), (1,)), ((), ()))
TN = (((0,), (0,)), ((), ()))
LANES = 128
VMEM_LIMIT = 48 * 2**20
VMEM_WHOLE = 60 * 2**20


def dot(a, b, dims=NN):
    return lax.dot_general(a, b, dims, preferred_element_type=f32)


def split(x):
    high = x.astype(bf16)
    return high, (x - high.astype(f32)).astype(bf16)


def dot_split(a, b, dims=NN):
    return dot(a, b[0], dims) + dot(a, b[1], dims)


def project_kernel(
    share, resid_ref, heads_ref, gain_ref, matrix_ref, down_ref, up_ref, out_ref, weights_ref
):
    rank, width = up_ref.shape[0], matrix_ref.shape[1]
    gain = gain_ref[...].astype(f32).reshape(1, -1)

    @pl.when(pl.program_id(0) == 0)
    def _():
        high, low = split(up_ref[...].astype(f32) * gain)
        weights_ref[:, :width] = dot(high, matrix_ref[...]) + dot(low, matrix_ref[...])
        gram = dot(up_ref[...], up_ref[...], NT)
        weights_ref[:, width:] = jnp.concatenate([gram, jnp.zeros_like(gram)], axis=1)

    resid = resid_ref[...]
    wide = resid.astype(f32)
    values = dot((wide * gain).astype(bf16), matrix_ref[...])
    small = [dot(heads_ref[...], down_ref[...], NT), dot(resid, up_ref[...], NT)]
    small = jnp.concatenate(small, axis=1)
    squares = jnp.sum(wide * wide, axis=1, keepdims=True)
    line = lax.broadcasted_iota(jnp.int32, (rank, share // 2), 0)
    diagonal = line[: share // 2] == lax.broadcasted_iota(jnp.int32, (share // 2, share // 2), 1)
    for piece in range(out_ref.shape[0]):
        rows = slice(piece * share, (piece + 1) * share)
        out_ref[piece, :share, :width] = values[rows].astype(bf16)
        out_ref[piece, :share, width:] = small[rows].astype(bf16)
        lines = jnp.zeros(line.shape, f32)
        for part in range(2):
            rows = slice(piece * share + part * (share // 2), piece * share + (part + 1) * (share // 2))
            across = jnp.sum(jnp.where(diagonal, squares[rows], 0.0), axis=0, keepdims=True)
            first = across.astype(bf16).astype(f32)
            lines = jnp.where(line == part, first, lines)
            lines = jnp.where(line == 2 + part, across - first, lines)
        blank = [jnp.zeros((rank, rank), f32), lines, jnp.zeros((rank, rank - share // 2), f32)]
        out_ref[piece, share:, :width] = weights_ref[:, :width].astype(bf16)
        tail = weights_ref[:, width:] + jnp.concatenate(blank, axis=1)
        out_ref[piece, share:, width:] = tail.astype(bf16)


def project(resid, heads, gain, matrix, down, up, share):
    tokens, features = resid.shape
    rank, width = up.shape[0], matrix.shape[1]
    pieces, group = tokens // share, 2
    rows, columns = group * share, width + 2 * rank
    whole = lambda i: (0, 0)
    return pl.pallas_call(
        functools.partial(project_kernel, share),
        grid=(pieces // group,),
        in_specs=[
            pl.BlockSpec((rows, features), lambda i: (i, 0)),
            pl.BlockSpec((rows, features), lambda i: (i, 0)),
            pl.BlockSpec((features,), lambda i: (0,)),
            pl.BlockSpec((features, width), whole),
            pl.BlockSpec(down.shape, whole),
            pl.BlockSpec(up.shape, whole),
        ],
        out_specs=pl.BlockSpec((group, share + rank, columns), lambda i: (i, 0, 0)),
        out_shape=jax.ShapeDtypeStruct((pieces, share + rank, columns), bf16),
        scratch_shapes=[pltpu.VMEM((rank, columns), f32)],
        compiler_params=pltpu.CompilerParams(vmem_limit_bytes=VMEM_WHOLE),
        cost_estimate=pl.CostEstimate(
            flops=2 * tokens * features * (width + 256),
            bytes_accessed=4 * tokens * features + 2 * features * width,
            transcendentals=0,
        ),
    )(resid, heads, gain, matrix, down, up)


def owner_kernel(loss_scale, pieces_ref, target_ref, values_ref, every_ref, sent_ref, sems):
    share, width = target_ref.shape
    tp = pieces_ref.shape[0]
    rank = pieces_ref.shape[1] - share
    total = functools.reduce(jnp.add, [pieces_ref[i].astype(f32) for i in range(tp)])
    through = split(total[share:, :width])
    gram = split(total[share:, width : width + rank])
    lines = total[share : share + 8, width + rank : width + rank + share // 2]
    lines = lines[0:2] + lines[2:4]
    diagonal = (share // 2, share // 2)
    diagonal = lax.broadcasted_iota(jnp.int32, diagonal, 0) == lax.broadcasted_iota(jnp.int32, diagonal, 1)
    squares = jnp.concatenate(
        [
            jnp.sum(jnp.where(diagonal, lines[i : i + 1], 0.0), axis=1, keepdims=True)
            for i in range(2)
        ],
        axis=0,
    )

    down_b = total[:share, width : width + rank].astype(bf16)
    down_wide = down_b.astype(f32)
    along = total[:share, width + rank :]
    hidden_up = along + 0.5 * dot_split(down_b, gram)
    squares = squares + 0.5 * jnp.sum(down_wide * (along + hidden_up), axis=1, keepdims=True)
    inverse_rms = lax.rsqrt(squares / MODEL_WIDTH + EPSILON)
    sums = inverse_rms * (total[:share, :width] + 0.5 * dot_split(down_b, through))
    values_ref[...] = sums.astype(bf16)
    error = (sums - target_ref[...].astype(f32)) * loss_scale
    inner = jnp.sum(error * sums, axis=1, keepdims=True) / MODEL_WIDTH
    high, low = split(error)
    down_grad = dot_split(high, through, NT) + dot(low, through[0], NT)
    down_grad = 0.5 * inverse_rms * (down_grad - inner * inverse_rms * hidden_up)
    weighted = down_wide * (inner * inverse_rms * inverse_rms)
    sent_ref[:, :width] = (error * inverse_rms).astype(bf16)
    sent_ref[:, width : width + 2 * rank] = jnp.concatenate([down_wide, down_grad], axis=1).astype(bf16)
    sent_ref[:, width + 2 * rank :] = weighted.astype(bf16)
    copies = [pltpu.make_async_copy(sent_ref, every_ref.at[i], sems.at[i]) for i in range(tp)]
    for copy in copies:
        copy.start()
    for copy in copies:
        copy.wait()


def owner(pieces, target, loss_scale):
    share, width = target.shape
    tp, rank = pieces.shape[0], pieces.shape[1] - share
    sent = (share, width + 3 * rank)
    vmem = pl.BlockSpec(memory_space=pltpu.VMEM)
    return pl.pallas_call(
        functools.partial(owner_kernel, loss_scale),
        in_specs=[vmem, vmem],
        out_specs=[vmem, pl.BlockSpec(memory_space=pl.ANY)],
        out_shape=[
            jax.ShapeDtypeStruct((share, width), bf16),
            jax.ShapeDtypeStruct((tp, *sent), bf16),
        ],
        scratch_shapes=[pltpu.VMEM(sent, bf16), pltpu.SemaphoreType.DMA((tp,))],
        compiler_params=pltpu.CompilerParams(vmem_limit_bytes=VMEM_LIMIT),
    )(pieces, target)


def gradients_kernel(
    z_size, core_ref, every_ref, resid_ref, heads_ref, up_ref, gain_ref, matrix_ref,
    kept_ref, small_ref, sent_ref, cross_ref,
):
    width = matrix_ref.shape[1]
    rank = up_ref.shape[0]
    error = every_ref[:, :width]
    down = every_ref[:, width : width + rank]

    @pl.when(pl.program_id(0) == 0)
    def _():
        high, low = split(dot(error, down, TN))
        cross_ref[0] = high
        cross_ref[1] = low

    core = core_ref[0]
    matrix = matrix_ref[...]
    hidden = lax.dot_general(up_ref[...], down, (((0,), (1,)), ((), ())), preferred_element_type=f32)
    hidden = (resid_ref[...].astype(f32) + 0.5 * hidden).astype(bf16)
    value = dot(hidden, error)
    a_part = dot(heads_ref[...], every_ref[:, width + rank : width + 2 * rank])
    b_part = dot(hidden, every_ref[:, width + 2 * rank :])
    crossed = dot(matrix, cross_ref[0]) + dot(matrix, cross_ref[1])
    b_part = 0.5 * (gain_ref[...] * crossed - b_part)
    small = jnp.concatenate([a_part, b_part], axis=1)
    gain_part = jnp.sum(value * matrix.astype(f32), axis=1, keepdims=True)
    group, own = kept_ref.shape[:2]
    lane = lax.broadcasted_iota(jnp.int32, small.shape, 1)
    line = lax.rem(lax.broadcasted_iota(jnp.int32, small.shape, 0), LANES)
    spread = jnp.where(lane == line, gain_part, 0.0).reshape(2 * group, own, LANES)
    gain_line = jnp.sum(spread, axis=1, keepdims=True)
    row = lax.broadcasted_iota(jnp.int32, (2 * group, own, LANES), 1)
    piece = pl.program_id(0) * group + lax.broadcasted_iota(jnp.int32, row.shape, 0) // 2
    gain_line = jnp.where(row == piece // z_size, gain_line, 0.0)
    small = jnp.concatenate([small.reshape(2 * group, own, -1), gain_line], axis=2)
    small = small.reshape(group, 2, own, -1)
    value = value.reshape(group, 2, own, width)
    first = core == 0
    kept_ref[...] = jnp.where(first, value[:, 0], value[:, 1]).astype(bf16)
    small_ref[...] = jnp.where(first, small[:, 0], small[:, 1])
    sent_ref[:, :, :width] = jnp.where(first, value[:, 1], value[:, 0]).astype(bf16)
    sent_ref[:, :, width:] = jnp.where(first, small[:, 1], small[:, 0]).astype(bf16)


def gradients(core, every, resid, heads, up, gain, matrix, own, z_size):
    features, tokens = resid.shape
    width, rank = matrix.shape[1], up.shape[0]
    block = 256
    pieces, group = features // (2 * own), block // (2 * own)
    shapes = [
        jax.ShapeDtypeStruct((pieces, own, width), bf16),
        jax.ShapeDtypeStruct((pieces, own, 2 * rank + LANES), f32),
        jax.ShapeDtypeStruct((pieces, own, width + 2 * rank + LANES), bf16),
    ]
    return pl.pallas_call(
        functools.partial(gradients_kernel, z_size),
        grid=(features // block,),
        in_specs=[
            pl.BlockSpec(memory_space=pltpu.SMEM),
            pl.BlockSpec(every.shape, lambda i: (0, 0)),
            pl.BlockSpec((block, tokens), lambda i: (i, 0)),
            pl.BlockSpec((block, tokens), lambda i: (i, 0)),
            pl.BlockSpec((rank, block), lambda i: (0, i)),
            pl.BlockSpec((block, 1), lambda i: (i, 0)),
            pl.BlockSpec((block, width), lambda i: (i, 0)),
        ],
        out_specs=[pl.BlockSpec((group, *s.shape[1:]), lambda i: (i, 0, 0)) for s in shapes],
        out_shape=shapes,
        scratch_shapes=[pltpu.VMEM((2, width, rank), bf16)],
        compiler_params=pltpu.CompilerParams(vmem_limit_bytes=VMEM_LIMIT),
        cost_estimate=pl.CostEstimate(
            flops=2 * tokens * features * (width + 4 * rank),
            bytes_accessed=4 * tokens * features + 8 * features * width,
            transcendentals=0,
        ),
    )(core, every, resid, heads, up, gain, matrix)


def assemble_kernel(core_ref, mine_ref, got_ref, a_ref, b_ref, gain_ref):
    z_size, own = mine_ref.shape[:2]
    rank, features = a_ref.shape
    together = LANES // (2 * own)
    first = core_ref[0] == 0
    for y in range(2):
        for start in range(0, z_size, together):
            lines, gain_line = [], jnp.zeros((1, LANES), f32)
            for z in range(start, start + together):
                mine = mine_ref[z].astype(f32)
                got = got_ref[z].astype(f32)
                lanes = slice(y * LANES, (y + 1) * LANES)
                lines += [
                    jnp.where(first, mine[:, lanes], got[:, lanes]),
                    jnp.where(first, got[:, lanes], mine[:, lanes]),
                ]
                gain_line += (mine + got)[y : y + 1, 2 * LANES :]
            both = jnp.concatenate(lines, axis=0).T
            place = y * (features // 2) + start * 2 * own
            a_ref[:, place : place + LANES] = both[:rank]
            b_ref[:, place : place + LANES] = both[rank:]
            gain_ref[:, place : place + LANES] = gain_line


def assemble(core, mine, got, rank):
    z_size, own = mine.shape[:2]
    features = 2 * z_size * 2 * own
    whole = jax.ShapeDtypeStruct((rank, features), f32)
    vmem = pl.BlockSpec(memory_space=pltpu.VMEM)
    return pl.pallas_call(
        assemble_kernel,
        in_specs=[pl.BlockSpec(memory_space=pltpu.SMEM), vmem, vmem],
        out_specs=[vmem, vmem, vmem],
        out_shape=[whole, whole, jax.ShapeDtypeStruct((1, features), f32)],
        compiler_params=pltpu.CompilerParams(vmem_limit_bytes=VMEM_LIMIT),
    )(core, mine, got)


def body(resid, heads, down_matrix, up, scale, value_matrix, target):
    share, width = target.shape
    tp = resid.shape[0] // share
    tokens = resid.shape[0] * lax.axis_size(ROWS)
    rank, features = up.shape
    core = lax.axis_index("core")
    gain = scale.astype(f32)

    pieces = project(resid, heads, scale, value_matrix, down_matrix.T, up, share)
    pieces = lax.all_to_all(pieces, TP, 0, 0, tiled=True)
    values, every = owner(pieces, target, 1.0 / tokens**0.5)
    every = lax.all_to_all(every, TP, 0, 0, tiled=True)
    every = every.reshape(tp * share, -1)

    y_size, z_size, core_size = (lax.axis_size(a) for a in ("y_hi", Z, "core"))
    own = features // (y_size * z_size * core_size)
    kept, small, sent = gradients(
        core.reshape(1), every, resid.T, heads.T, up, gain[:, None], value_matrix, own, z_size
    )

    got = swap(sent, "core")
    small = (small + got[:, :, width:].astype(f32)).astype(bf16)
    small = small.reshape(y_size, z_size, own, -1)
    gains = small[0, :, :8, 2 * rank :] + small[1, :, :8, 2 * rank :]
    small = small[..., : 2 * rank].transpose(1, 0, 2, 3).reshape(z_size, y_size * own, -1)
    small = jnp.concatenate([small, gains], axis=1)
    small = lax.all_to_all(small, Z, 0, 0, tiled=True)

    half, got = width // 2, got[:, :, :width]
    odd, me = lax.axis_index("z_odd"), lax.axis_index("y_hi")
    columns = lambda x, i: lax.dynamic_slice_in_dim(x, i * half, half, 2).astype(f32)
    other = swap((columns(kept, 1 - odd) + columns(got, 1 - odd)).astype(bf16), "z_odd")
    value = columns(kept, odd) + columns(got, odd) + other.astype(f32)
    value = value.reshape(y_size, z_size, own, half)
    rows = lambda x, i: lax.dynamic_index_in_dim(x, i, 0, keepdims=False)
    other = swap(rows(value, 1 - me).astype(bf16), "y_hi")
    value = (rows(value, me) + other.astype(f32)).astype(bf16)

    small = jnp.sum(small.astype(f32), axis=0)
    small = (small + swap(small, "y_hi")).astype(bf16)

    gains = jnp.pad(small[y_size * own :], ((0, own - 8), (0, 0)))
    small = [small[i * own : (i + 1) * own] for i in range(y_size)]
    small = jnp.concatenate([*small, gains], axis=1)
    small = jnp.broadcast_to(small, (z_size, *small.shape))
    value = lax.all_to_all(jnp.concatenate([value, small], axis=2), Z, 0, 0, tiled=True)
    small = value[:, :, half:]
    a_grad, b_grad, gain_grad = assemble(core.reshape(1), small, swap(small, "core"), rank)

    value = value[:, :, :half].astype(f32).reshape(-1, 2, own, half)
    value = jnp.concatenate([*jnp.sum(value, axis=0)], axis=1)
    own_gain = lax.dynamic_slice_in_dim(gain, lax.axis_index(ROWS) * own, own, 0)
    value_grad = (value * own_gain[:, None]).astype(bf16)
    return (values, value_grad, a_grad.T, b_grad, gain_grad.reshape(-1))


def swap(x, axis):
    return lax.ppermute(x, axis, [(0, 1), (1, 0)])


def solution(mesh):
    rows, tp = mesh.shape["rows"], mesh.shape["tp"]
    y_hi, z_odd, core, y_lo = 2, 2, 2, 2
    z_pair = rows // (y_hi * z_odd * core)
    fine = Mesh(
        mesh.devices.reshape(y_hi, z_pair, z_odd, core, tp // y_lo, y_lo), (*ROWS, *TP)
    )
    in_specs = (
        P(ROWS, TP),
        P(ROWS, TP),
        P(TP, None),
        P(None, TP),
        P(TP),
        P(TP, None),
        P((*ROWS, *TP), None),
    )
    out_specs = (
        P((*ROWS, *TP), None),
        P((*TP, *ROWS), None),
        P(TP, None),
        P(None, TP),
        P(TP),
    )
    return jax.shard_map(body, mesh=fine, in_specs=in_specs, out_specs=out_specs, check_vma=False)
```

```python
import functools

import jax
import jax.numpy as jnp
from jax import lax
from jax.experimental import pallas as pl
from jax.experimental.pallas import tpu as pltpu
from jax.sharding import Mesh, PartitionSpec as P

MODEL_WIDTH = 8192
EPSILON = 1e-06
TP = ("x", "y_lo")
Z = ("z_pair", "z_odd")
ROWS = ("y_hi", *Z, "core")
bf16 = jnp.bfloat16
f32 = jnp.float32
NN = (((1,), (0,)), ((), ()))
NT = (((1,), (1,)), ((), ()))
TN = (((0,), (0,)), ((), ()))
LANES = 128
VMEM_LIMIT = 48 * 2**20
VMEM_WHOLE = 60 * 2**20
VMEM_SOME = 16 * 2**20


def dot(a, b, dims=NN):
    return lax.dot_general(a, b, dims, preferred_element_type=f32)


def split(x):
    high = x.astype(bf16)
    return high, (x - high.astype(f32)).astype(bf16)


def dot_split(a, b, dims=NN):
    return dot(a, b[0], dims) + dot(a, b[1], dims)


def project_kernel(
    share, resid_ref, heads_ref, gain_ref, matrix_ref, down_ref, up_ref, out_ref, weights_ref
):
    rank, width = up_ref.shape[0], matrix_ref.shape[1]
    gain = gain_ref[...].astype(f32).reshape(1, -1)

    @pl.when(pl.program_id(0) == 0)
    def _():
        high, low = split(up_ref[...].astype(f32) * gain)
        weights_ref[:, :width] = dot(high, matrix_ref[...]) + dot(low, matrix_ref[...])
        gram = dot(up_ref[...], up_ref[...], NT)
        weights_ref[:, width:] = jnp.concatenate([gram, jnp.zeros_like(gram)], axis=1)

    resid = resid_ref[...]
    wide = resid.astype(f32)
    values = dot((wide * gain).astype(bf16), matrix_ref[...])
    small = [dot(heads_ref[...], down_ref[...], NT), dot(resid, up_ref[...], NT)]
    small = jnp.concatenate(small, axis=1)
    squares = jnp.sum(wide * wide, axis=1, keepdims=True)
    line = lax.broadcasted_iota(jnp.int32, (rank, share // 2), 0)
    diagonal = line[: share // 2] == lax.broadcasted_iota(jnp.int32, (share // 2, share // 2), 1)
    for piece in range(out_ref.shape[0]):
        rows = slice(piece * share, (piece + 1) * share)
        out_ref[piece, :share, :width] = values[rows].astype(bf16)
        out_ref[piece, :share, width:] = small[rows].astype(bf16)
        lines = jnp.zeros(line.shape, f32)
        for part in range(2):
            rows = slice(piece * share + part * (share // 2), piece * share + (part + 1) * (share // 2))
            across = jnp.sum(jnp.where(diagonal, squares[rows], 0.0), axis=0, keepdims=True)
            first = across.astype(bf16).astype(f32)
            lines = jnp.where(line == part, first, lines)
            lines = jnp.where(line == 2 + part, across - first, lines)
        blank = [jnp.zeros((rank, rank), f32), lines, jnp.zeros((rank, rank - share // 2), f32)]
        out_ref[piece, share:, :width] = weights_ref[:, :width].astype(bf16)
        tail = weights_ref[:, width:] + jnp.concatenate(blank, axis=1)
        out_ref[piece, share:, width:] = tail.astype(bf16)


def project(resid, heads, gain, matrix, down, up, share):
    tokens, features = resid.shape
    rank, width = up.shape[0], matrix.shape[1]
    pieces, group = tokens // share, 4
    rows, columns = group * share, width + 2 * rank
    whole = lambda i: (0, 0)
    return pl.pallas_call(
        functools.partial(project_kernel, share),
        grid=(pieces // group,),
        in_specs=[
            pl.BlockSpec((rows, features), lambda i: (i, 0)),
            pl.BlockSpec((rows, features), lambda i: (i, 0)),
            pl.BlockSpec((features,), lambda i: (0,)),
            pl.BlockSpec((features, width), whole),
            pl.BlockSpec(down.shape, whole),
            pl.BlockSpec(up.shape, whole),
        ],
        out_specs=pl.BlockSpec((group, share + rank, columns), lambda i: (i, 0, 0)),
        out_shape=jax.ShapeDtypeStruct((pieces, share + rank, columns), bf16),
        scratch_shapes=[pltpu.VMEM((rank, columns), f32)],
        compiler_params=pltpu.CompilerParams(vmem_limit_bytes=VMEM_WHOLE),
        cost_estimate=pl.CostEstimate(
            flops=2 * tokens * features * (width + 256),
            bytes_accessed=4 * tokens * features + 2 * features * width,
            transcendentals=0,
        ),
    )(resid, heads, gain, matrix, down, up)


def owner_kernel(loss_scale, pieces_ref, target_ref, values_ref, every_ref, sent_ref, sems):
    share, width = target_ref.shape
    tp = pieces_ref.shape[0]
    rank = pieces_ref.shape[1] - share
    total = functools.reduce(jnp.add, [pieces_ref[i].astype(f32) for i in range(tp)])
    through = split(total[share:, :width])
    gram = split(total[share:, width : width + rank])
    lines = total[share : share + 8, width + rank : width + rank + share // 2]
    lines = lines[0:2] + lines[2:4]
    diagonal = (share // 2, share // 2)
    diagonal = lax.broadcasted_iota(jnp.int32, diagonal, 0) == lax.broadcasted_iota(jnp.int32, diagonal, 1)
    squares = jnp.concatenate(
        [
            jnp.sum(jnp.where(diagonal, lines[i : i + 1], 0.0), axis=1, keepdims=True)
            for i in range(2)
        ],
        axis=0,
    )

    down_b = total[:share, width : width + rank].astype(bf16)
    down_wide = down_b.astype(f32)
    along = total[:share, width + rank :]
    hidden_up = along + 0.5 * dot_split(down_b, gram)
    squares = squares + 0.5 * jnp.sum(down_wide * (along + hidden_up), axis=1, keepdims=True)
    inverse_rms = lax.rsqrt(squares / MODEL_WIDTH + EPSILON)
    sums = inverse_rms * (total[:share, :width] + 0.5 * dot_split(down_b, through))
    values_ref[...] = sums.astype(bf16)
    error = (sums - target_ref[...].astype(f32)) * loss_scale
    inner = jnp.sum(error * sums, axis=1, keepdims=True) / MODEL_WIDTH
    high, low = split(error)
    down_grad = dot_split(high, through, NT) + dot(low, through[0], NT)
    down_grad = 0.5 * inverse_rms * (down_grad - inner * inverse_rms * hidden_up)
    weighted = down_wide * (inner * inverse_rms * inverse_rms)
    sent_ref[:, :width] = (error * inverse_rms).astype(bf16)
    sent_ref[:, width : width + 2 * rank] = jnp.concatenate([down_wide, down_grad], axis=1).astype(bf16)
    sent_ref[:, width + 2 * rank :] = weighted.astype(bf16)
    copies = [pltpu.make_async_copy(sent_ref, every_ref.at[i], sems.at[i]) for i in range(tp)]
    for copy in copies:
        copy.start()
    for copy in copies:
        copy.wait()


def owner(pieces, target, loss_scale):
    share, width = target.shape
    tp, rank = pieces.shape[0], pieces.shape[1] - share
    sent = (share, width + 3 * rank)
    vmem = pl.BlockSpec(memory_space=pltpu.VMEM)
    return pl.pallas_call(
        functools.partial(owner_kernel, loss_scale),
        in_specs=[vmem, vmem],
        out_specs=[vmem, pl.BlockSpec(memory_space=pl.ANY)],
        out_shape=[
            jax.ShapeDtypeStruct((share, width), bf16),
            jax.ShapeDtypeStruct((tp, *sent), bf16),
        ],
        scratch_shapes=[pltpu.VMEM(sent, bf16), pltpu.SemaphoreType.DMA((tp,))],
        compiler_params=pltpu.CompilerParams(vmem_limit_bytes=VMEM_LIMIT),
    )(pieces, target)


def gradients_kernel(
    z_size, core_ref, every_ref, resid_ref, heads_ref, up_ref, gain_ref, matrix_ref,
    kept_ref, small_ref, sent_ref, cross_ref,
):
    width = matrix_ref.shape[1]
    rank = up_ref.shape[0]
    error = every_ref[:, :width]
    down = every_ref[:, width : width + rank]

    @pl.when(pl.program_id(0) == 0)
    def _():
        high, low = split(dot(error, down, TN))
        cross_ref[0] = high
        cross_ref[1] = low

    core = core_ref[0]
    matrix = matrix_ref[...]
    hidden = lax.dot_general(up_ref[...], down, (((0,), (1,)), ((), ())), preferred_element_type=f32)
    hidden = (resid_ref[...].astype(f32) + 0.5 * hidden).astype(bf16)
    value = dot(hidden, error)
    a_part = dot(heads_ref[...], every_ref[:, width + rank : width + 2 * rank])
    b_part = dot(hidden, every_ref[:, width + 2 * rank :])
    crossed = dot(matrix, cross_ref[0]) + dot(matrix, cross_ref[1])
    b_part = 0.5 * (gain_ref[...] * crossed - b_part)
    small = jnp.concatenate([a_part, b_part], axis=1)
    gain_part = jnp.sum(value * matrix.astype(f32), axis=1, keepdims=True)
    group, own = kept_ref.shape[:2]
    lane = lax.broadcasted_iota(jnp.int32, small.shape, 1)
    line = lax.rem(lax.broadcasted_iota(jnp.int32, small.shape, 0), LANES)
    spread = jnp.where(lane == line, gain_part, 0.0).reshape(2 * group, own, LANES)
    gain_line = jnp.sum(spread, axis=1, keepdims=True)
    row = lax.broadcasted_iota(jnp.int32, (2 * group, own, LANES), 1)
    piece = pl.program_id(0) * group + lax.broadcasted_iota(jnp.int32, row.shape, 0) // 2
    gain_line = jnp.where(row == piece // z_size, gain_line, 0.0)
    small = jnp.concatenate([small.reshape(2 * group, own, -1), gain_line], axis=2)
    small = small.reshape(group, 2, own, -1)
    value = value.reshape(group, 2, own, width)
    first = core == 0
    kept_ref[...] = jnp.where(first, value[:, 0], value[:, 1]).astype(bf16)
    small_ref[...] = jnp.where(first, small[:, 0], small[:, 1])
    sent_ref[:, :, :width] = jnp.where(first, value[:, 1], value[:, 0]).astype(bf16)
    sent_ref[:, :, width:] = jnp.where(first, small[:, 1], small[:, 0]).astype(bf16)


def gradients(core, every, resid, heads, up, gain, matrix, own, z_size):
    features, tokens = resid.shape
    width, rank = matrix.shape[1], up.shape[0]
    block = 512
    pieces, group = features // (2 * own), block // (2 * own)
    shapes = [
        jax.ShapeDtypeStruct((pieces, own, width), bf16),
        jax.ShapeDtypeStruct((pieces, own, 2 * rank + LANES), f32),
        jax.ShapeDtypeStruct((pieces, own, width + 2 * rank + LANES), bf16),
    ]
    return pl.pallas_call(
        functools.partial(gradients_kernel, z_size),
        grid=(features // block,),
        in_specs=[
            pl.BlockSpec(memory_space=pltpu.SMEM),
            pl.BlockSpec(every.shape, lambda i: (0, 0)),
            pl.BlockSpec((block, tokens), lambda i: (i, 0)),
            pl.BlockSpec((block, tokens), lambda i: (i, 0)),
            pl.BlockSpec((rank, block), lambda i: (0, i)),
            pl.BlockSpec((block, 1), lambda i: (i, 0)),
            pl.BlockSpec((block, width), lambda i: (i, 0)),
        ],
        out_specs=[pl.BlockSpec((group, *s.shape[1:]), lambda i: (i, 0, 0)) for s in shapes],
        out_shape=shapes,
        scratch_shapes=[pltpu.VMEM((2, width, rank), bf16)],
        compiler_params=pltpu.CompilerParams(vmem_limit_bytes=VMEM_LIMIT),
        cost_estimate=pl.CostEstimate(
            flops=2 * tokens * features * (width + 4 * rank),
            bytes_accessed=4 * tokens * features + 8 * features * width,
            transcendentals=0,
        ),
    )(core, every, resid, heads, up, gain, matrix)


def small_kernel(small_ref, got_ref, out_ref):
    z_size = out_ref.shape[0]
    y_size = small_ref.shape[0] // z_size
    small = small_ref[...] + got_ref[...].astype(f32)
    for z in range(z_size):
        places = [y * z_size + z for y in range(y_size)]
        lines = [small[i, :, :LANES] for i in places]
        gains = functools.reduce(jnp.add, [small[i, :8, LANES:] for i in places])
        out_ref[z] = jnp.concatenate([*lines, gains], axis=0).astype(bf16)


def small_pieces(small, got, y_size):
    pieces, own, columns = small.shape
    z_size = pieces // y_size
    last = got.shape[2] // columns - 1
    return pl.pallas_call(
        small_kernel,
        grid=(1,),
        in_specs=[
            pl.BlockSpec(small.shape, lambda i: (0, 0, 0)),
            pl.BlockSpec(small.shape, lambda i: (0, 0, last)),
        ],
        out_specs=pl.BlockSpec((z_size, y_size * own + 8, LANES), lambda i: (0, 0, 0)),
        out_shape=jax.ShapeDtypeStruct((z_size, y_size * own + 8, LANES), bf16),
        compiler_params=pltpu.CompilerParams(vmem_limit_bytes=VMEM_SOME),
    )(small, got)


def assemble_kernel(core_ref, mine_ref, got_ref, a_ref, b_ref, gain_ref):
    z_size, own = mine_ref.shape[:2]
    rank, features = a_ref.shape
    together = LANES // (2 * own)
    first = core_ref[0] == 0
    for y in range(2):
        for start in range(0, z_size, together):
            lines, gain_line = [], jnp.zeros((1, LANES), f32)
            for z in range(start, start + together):
                mine = mine_ref[z].astype(f32)
                got = got_ref[z].astype(f32)
                lanes = slice(y * LANES, (y + 1) * LANES)
                lines += [
                    jnp.where(first, mine[:, lanes], got[:, lanes]),
                    jnp.where(first, got[:, lanes], mine[:, lanes]),
                ]
                gain_line += (mine + got)[y : y + 1, 2 * LANES :]
            both = jnp.concatenate(lines, axis=0).T
            place = y * (features // 2) + start * 2 * own
            a_ref[:, place : place + LANES] = both[:rank]
            b_ref[:, place : place + LANES] = both[rank:]
            gain_ref[:, place : place + LANES] = gain_line


def assemble(core, mine, got, rank):
    z_size, own = mine.shape[:2]
    features = 2 * z_size * 2 * own
    whole = jax.ShapeDtypeStruct((rank, features), f32)
    vmem = pl.BlockSpec(memory_space=pltpu.VMEM)
    return pl.pallas_call(
        assemble_kernel,
        in_specs=[pl.BlockSpec(memory_space=pltpu.SMEM), vmem, vmem],
        out_specs=[vmem, vmem, vmem],
        out_shape=[whole, whole, jax.ShapeDtypeStruct((1, features), f32)],
        compiler_params=pltpu.CompilerParams(vmem_limit_bytes=VMEM_LIMIT),
    )(core, mine, got)


def body(resid, heads, down_matrix, up, scale, value_matrix, target):
    share, width = target.shape
    tp = resid.shape[0] // share
    tokens = resid.shape[0] * lax.axis_size(ROWS)
    rank, features = up.shape
    core = lax.axis_index("core")
    gain = scale.astype(f32)

    pieces = project(resid, heads, scale, value_matrix, down_matrix.T, up, share)
    pieces = lax.all_to_all(pieces, TP, 0, 0, tiled=True)
    values, every = owner(pieces, target, 1.0 / tokens**0.5)
    every = lax.all_to_all(every, TP, 0, 0, tiled=True)
    every = every.reshape(tp * share, -1)

    y_size, z_size, core_size = (lax.axis_size(a) for a in ("y_hi", Z, "core"))
    own = features // (y_size * z_size * core_size)
    kept, small, sent = gradients(
        core.reshape(1), every, resid.T, heads.T, up, gain[:, None], value_matrix, own, z_size
    )

    got = swap(sent, "core")
    small = small_pieces(small, got, y_size)
    small = lax.all_to_all(small, Z, 0, 0, tiled=True)

    half, got = width // 2, got[:, :, :width]
    odd, me = lax.axis_index("z_odd"), lax.axis_index("y_hi")

    def quarter(y, z):
        parts = [x.reshape(y_size, z_size, own, width) for x in (kept, got)]
        parts = [lax.dynamic_index_in_dim(x, y, 0, keepdims=False) for x in parts]
        parts = [lax.dynamic_slice_in_dim(x, z * half, half, 2) for x in parts]
        return parts[0].astype(f32) + parts[1].astype(f32)

    value = quarter(me, odd)
    for y, z, axis in (
        (me, 1 - odd, "z_odd"),
        (1 - me, odd, "y_hi"),
        (1 - me, 1 - odd, ("y_hi", "z_odd")),
    ):
        value = value + swap(quarter(y, z).astype(bf16), axis).astype(f32)
    value = value.astype(bf16)

    small = jnp.sum(small.astype(f32), axis=0)
    small = (small + swap(small, "y_hi")).astype(bf16)

    gains = jnp.pad(small[y_size * own :], ((0, own - 8), (0, 0)))
    small = [small[i * own : (i + 1) * own] for i in range(y_size)]
    small = jnp.concatenate([*small, gains], axis=1)
    small = jnp.broadcast_to(small, (z_size, *small.shape))
    value = lax.all_to_all(jnp.concatenate([value, small], axis=2), Z, 0, 0, tiled=True)
    small = value[:, :, half:]
    a_grad, b_grad, gain_grad = assemble(core.reshape(1), small, swap(small, "core"), rank)

    value = value[:, :, :half].astype(f32).reshape(-1, 2, own, half)
    value = jnp.concatenate([*jnp.sum(value, axis=0)], axis=1)
    own_gain = lax.dynamic_slice_in_dim(gain, lax.axis_index(ROWS) * own, own, 0)
    value_grad = (value * own_gain[:, None]).astype(bf16)
    return (values, value_grad, a_grad.T, b_grad, gain_grad.reshape(-1))


def swap(x, axis):
    last = lax.axis_size(axis) - 1
    return lax.ppermute(x, axis, [(i, last - i) for i in range(last + 1)])


def solution(mesh):
    rows, tp = mesh.shape["rows"], mesh.shape["tp"]
    y_hi, z_odd, core, y_lo = 2, 2, 2, 2
    z_pair = rows // (y_hi * z_odd * core)
    fine = Mesh(
        mesh.devices.reshape(y_hi, z_pair, z_odd, core, tp // y_lo, y_lo), (*ROWS, *TP)
    )
    in_specs = (
        P(ROWS, TP),
        P(ROWS, TP),
        P(TP, None),
        P(None, TP),
        P(TP),
        P(TP, None),
        P((*ROWS, *TP), None),
    )
    out_specs = (
        P((*ROWS, *TP), None),
        P((*TP, *ROWS), None),
        P(TP, None),
        P(None, TP),
        P(TP),
    )
    return jax.shard_map(body, mesh=fine, in_specs=in_specs, out_specs=out_specs, check_vma=False)
```

```python
import functools

import jax
import jax.numpy as jnp
from jax import lax
from jax.experimental import pallas as pl
from jax.experimental.pallas import tpu as pltpu
from jax.sharding import Mesh, PartitionSpec as P

MODEL_WIDTH = 8192
EPSILON = 1e-06
TP = ("x", "y_lo")
Z = ("z_pair", "z_odd")
ROWS = ("y_hi", *Z, "core")
bf16 = jnp.bfloat16
f32 = jnp.float32
NN = (((1,), (0,)), ((), ()))
NT = (((1,), (1,)), ((), ()))
TN = (((0,), (0,)), ((), ()))
LANES = 128
VMEM_LIMIT = 48 * 2**20
VMEM_WHOLE = 60 * 2**20
VMEM_SOME = 16 * 2**20


def dot(a, b, dims=NN):
    return lax.dot_general(a, b, dims, preferred_element_type=f32)


def split(x):
    high = x.astype(bf16)
    return high, (x - high.astype(f32)).astype(bf16)


def dot_split(a, b, dims=NN):
    return dot(a, b[0], dims) + dot(a, b[1], dims)


def project_kernel(
    share, resid_ref, heads_ref, gain_ref, matrix_ref, down_ref, up_ref, out_ref, weights_ref
):
    rank, width = up_ref.shape[0], matrix_ref.shape[1]
    gain = gain_ref[...].astype(f32).reshape(1, -1)

    @pl.when(pl.program_id(0) == 0)
    def _():
        high, low = split(up_ref[...].astype(f32) * gain)
        weights_ref[:, :width] = dot(high, matrix_ref[...]) + dot(low, matrix_ref[...])
        gram = dot(up_ref[...], up_ref[...], NT)
        weights_ref[:, width:] = jnp.concatenate([gram, jnp.zeros_like(gram)], axis=1)

    resid = resid_ref[...]
    wide = resid.astype(f32)
    values = dot((wide * gain).astype(bf16), matrix_ref[...])
    small = [dot(heads_ref[...], down_ref[...], NT), dot(resid, up_ref[...], NT)]
    small = jnp.concatenate(small, axis=1)
    squares = jnp.sum(wide * wide, axis=1, keepdims=True)
    line = lax.broadcasted_iota(jnp.int32, (rank, share // 2), 0)
    diagonal = line[: share // 2] == lax.broadcasted_iota(jnp.int32, (share // 2, share // 2), 1)
    for piece in range(out_ref.shape[0]):
        rows = slice(piece * share, (piece + 1) * share)
        out_ref[piece, :share, :width] = values[rows].astype(bf16)
        out_ref[piece, :share, width:] = small[rows].astype(bf16)
        lines = jnp.zeros(line.shape, f32)
        for part in range(2):
            rows = slice(piece * share + part * (share // 2), piece * share + (part + 1) * (share // 2))
            across = jnp.sum(jnp.where(diagonal, squares[rows], 0.0), axis=0, keepdims=True)
            first = across.astype(bf16).astype(f32)
            lines = jnp.where(line == part, first, lines)
            lines = jnp.where(line == 2 + part, across - first, lines)
        blank = [jnp.zeros((rank, rank), f32), lines, jnp.zeros((rank, rank - share // 2), f32)]
        out_ref[piece, share:, :width] = weights_ref[:, :width].astype(bf16)
        tail = weights_ref[:, width:] + jnp.concatenate(blank, axis=1)
        out_ref[piece, share:, width:] = tail.astype(bf16)


def project(resid, heads, gain, matrix, down, up, share):
    tokens, features = resid.shape
    rank, width = up.shape[0], matrix.shape[1]
    pieces, group = tokens // share, 4
    rows, columns = group * share, width + 2 * rank
    whole = lambda i: (0, 0)
    return pl.pallas_call(
        functools.partial(project_kernel, share),
        grid=(pieces // group,),
        in_specs=[
            pl.BlockSpec((rows, features), lambda i: (i, 0)),
            pl.BlockSpec((rows, features), lambda i: (i, 0)),
            pl.BlockSpec((features,), lambda i: (0,)),
            pl.BlockSpec((features, width), whole),
            pl.BlockSpec(down.shape, whole),
            pl.BlockSpec(up.shape, whole),
        ],
        out_specs=pl.BlockSpec((group, share + rank, columns), lambda i: (i, 0, 0)),
        out_shape=jax.ShapeDtypeStruct((pieces, share + rank, columns), bf16),
        scratch_shapes=[pltpu.VMEM((rank, columns), f32)],
        compiler_params=pltpu.CompilerParams(vmem_limit_bytes=VMEM_WHOLE),
        cost_estimate=pl.CostEstimate(
            flops=2 * tokens * features * (width + 256),
            bytes_accessed=4 * tokens * features + 2 * features * width,
            transcendentals=0,
        ),
    )(resid, heads, gain, matrix, down, up)


def owner_kernel(loss_scale, pieces_ref, target_ref, values_ref, every_ref):
    share, width = target_ref.shape
    tp = pieces_ref.shape[0]
    rank = pieces_ref.shape[1] - share
    total = functools.reduce(jnp.add, [pieces_ref[i].astype(f32) for i in range(tp)])
    through = split(total[share:, :width])
    gram = split(total[share:, width : width + rank])
    lines = total[share : share + 8, width + rank : width + rank + share // 2]
    lines = lines[0:2] + lines[2:4]
    diagonal = (share // 2, share // 2)
    diagonal = lax.broadcasted_iota(jnp.int32, diagonal, 0) == lax.broadcasted_iota(jnp.int32, diagonal, 1)
    squares = jnp.concatenate(
        [
            jnp.sum(jnp.where(diagonal, lines[i : i + 1], 0.0), axis=1, keepdims=True)
            for i in range(2)
        ],
        axis=0,
    )

    down_b = total[:share, width : width + rank].astype(bf16)
    down_wide = down_b.astype(f32)
    along = total[:share, width + rank :]
    hidden_up = along + 0.5 * dot_split(down_b, gram)
    squares = squares + 0.5 * jnp.sum(down_wide * (along + hidden_up), axis=1, keepdims=True)
    inverse_rms = lax.rsqrt(squares / MODEL_WIDTH + EPSILON)
    sums = inverse_rms * (total[:share, :width] + 0.5 * dot_split(down_b, through))
    values_ref[...] = sums.astype(bf16)
    error = (sums - target_ref[...].astype(f32)) * loss_scale
    inner = jnp.sum(error * sums, axis=1, keepdims=True) / MODEL_WIDTH
    high, low = split(error)
    down_grad = dot_split(high, through, NT) + dot(low, through[0], NT)
    down_grad = 0.5 * inverse_rms * (down_grad - inner * inverse_rms * hidden_up)
    weighted = down_wide * (inner * inverse_rms * inverse_rms)
    small = jnp.concatenate([down_wide, down_grad], axis=1).astype(bf16)
    error, weighted = (error * inverse_rms).astype(bf16), weighted.astype(bf16)
    for i in range(tp):
        every_ref[i, :, :width] = error
        every_ref[i, :, width : width + 2 * rank] = small
        every_ref[i, :, width + 2 * rank :] = weighted


def owner(pieces, target, loss_scale):
    share, width = target.shape
    tp, rank = pieces.shape[0], pieces.shape[1] - share
    sent = (share, width + 3 * rank)
    vmem = pl.BlockSpec(memory_space=pltpu.VMEM)
    return pl.pallas_call(
        functools.partial(owner_kernel, loss_scale),
        in_specs=[vmem, vmem],
        out_specs=[vmem, vmem],
        out_shape=[
            jax.ShapeDtypeStruct((share, width), bf16),
            jax.ShapeDtypeStruct((tp, *sent), bf16),
        ],
        compiler_params=pltpu.CompilerParams(vmem_limit_bytes=VMEM_SOME),
    )(pieces, target)


def gradients_kernel(
    z_size, core_ref, every_ref, resid_ref, heads_ref, up_ref, gain_ref, matrix_ref,
    kept_ref, small_ref, sent_ref, cross_ref,
):
    width = matrix_ref.shape[1]
    rank = up_ref.shape[0]
    error = every_ref[:, :width]
    down = every_ref[:, width : width + rank]

    @pl.when(pl.program_id(0) == 0)
    def _():
        high, low = split(dot(error, down, TN))
        cross_ref[0] = high
        cross_ref[1] = low

    core = core_ref[0]
    matrix = matrix_ref[...]
    hidden = lax.dot_general(up_ref[...], down, (((0,), (1,)), ((), ())), preferred_element_type=f32)
    hidden = (resid_ref[...].astype(f32) + 0.5 * hidden).astype(bf16)
    value = dot(hidden, error)
    a_part = dot(heads_ref[...], every_ref[:, width + rank : width + 2 * rank])
    b_part = dot(hidden, every_ref[:, width + 2 * rank :])
    crossed = dot(matrix, cross_ref[0]) + dot(matrix, cross_ref[1])
    b_part = 0.5 * (gain_ref[...] * crossed - b_part)
    small = jnp.concatenate([a_part, b_part], axis=1)
    gain_part = jnp.sum(value * matrix.astype(f32), axis=1, keepdims=True)
    group, own = kept_ref.shape[:2]
    lane = lax.broadcasted_iota(jnp.int32, small.shape, 1)
    line = lax.rem(lax.broadcasted_iota(jnp.int32, small.shape, 0), LANES)
    spread = jnp.where(lane == line, gain_part, 0.0).reshape(2 * group, own, LANES)
    gain_line = jnp.sum(spread, axis=1, keepdims=True)
    row = lax.broadcasted_iota(jnp.int32, (2 * group, own, LANES), 1)
    piece = pl.program_id(0) * group + lax.broadcasted_iota(jnp.int32, row.shape, 0) // 2
    gain_line = jnp.where(row == piece // z_size, gain_line, 0.0)
    small = jnp.concatenate([small.reshape(2 * group, own, -1), gain_line], axis=2)
    small = small.reshape(group, 2, own, -1)
    value = value.reshape(group, 2, own, width)
    first = core == 0
    kept_ref[...] = jnp.where(first, value[:, 0], value[:, 1]).astype(bf16)
    small_ref[...] = jnp.where(first, small[:, 0], small[:, 1])
    sent_ref[:, :, :width] = jnp.where(first, value[:, 1], value[:, 0]).astype(bf16)
    sent_ref[:, :, width:] = jnp.where(first, small[:, 1], small[:, 0]).astype(bf16)


def gradients(core, every, resid, heads, up, gain, matrix, own, z_size):
    features, tokens = resid.shape
    width, rank = matrix.shape[1], up.shape[0]
    block = 512
    pieces, group = features // (2 * own), block // (2 * own)
    shapes = [
        jax.ShapeDtypeStruct((pieces, own, width), bf16),
        jax.ShapeDtypeStruct((pieces, own, 2 * rank + LANES), f32),
        jax.ShapeDtypeStruct((pieces, own, width + 2 * rank + LANES), bf16),
    ]
    return pl.pallas_call(
        functools.partial(gradients_kernel, z_size),
        grid=(features // block,),
        in_specs=[
            pl.BlockSpec(memory_space=pltpu.SMEM),
            pl.BlockSpec(every.shape, lambda i: (0, 0)),
            pl.BlockSpec((block, tokens), lambda i: (i, 0)),
            pl.BlockSpec((block, tokens), lambda i: (i, 0)),
            pl.BlockSpec((rank, block), lambda i: (0, i)),
            pl.BlockSpec((block, 1), lambda i: (i, 0)),
            pl.BlockSpec((block, width), lambda i: (i, 0)),
        ],
        out_specs=[pl.BlockSpec((group, *s.shape[1:]), lambda i: (i, 0, 0)) for s in shapes],
        out_shape=shapes,
        scratch_shapes=[pltpu.VMEM((2, width, rank), bf16)],
        compiler_params=pltpu.CompilerParams(vmem_limit_bytes=VMEM_LIMIT),
        cost_estimate=pl.CostEstimate(
            flops=2 * tokens * features * (width + 4 * rank),
            bytes_accessed=4 * tokens * features + 8 * features * width,
            transcendentals=0,
        ),
    )(core, every, resid, heads, up, gain, matrix)


def small_kernel(small_ref, got_ref, out_ref):
    z_size = out_ref.shape[0]
    y_size = small_ref.shape[0] // z_size
    small = small_ref[...] + got_ref[...].astype(f32)
    for z in range(z_size):
        places = [y * z_size + z for y in range(y_size)]
        lines = [small[i, :, :LANES] for i in places]
        gains = functools.reduce(jnp.add, [small[i, :8, LANES:] for i in places])
        out_ref[z] = jnp.concatenate([*lines, gains], axis=0).astype(bf16)


def small_pieces(small, got, y_size):
    pieces, own, columns = small.shape
    z_size = pieces // y_size
    last = got.shape[2] // columns - 1
    return pl.pallas_call(
        small_kernel,
        grid=(1,),
        in_specs=[
            pl.BlockSpec(small.shape, lambda i: (0, 0, 0)),
            pl.BlockSpec(small.shape, lambda i: (0, 0, last)),
        ],
        out_specs=pl.BlockSpec((z_size, y_size * own + 8, LANES), lambda i: (0, 0, 0)),
        out_shape=jax.ShapeDtypeStruct((z_size, y_size * own + 8, LANES), bf16),
        compiler_params=pltpu.CompilerParams(vmem_limit_bytes=VMEM_SOME),
    )(small, got)


def assemble_kernel(own, core_ref, mine_ref, got_ref, a_ref, b_ref, gain_ref):
    z_size = mine_ref.shape[0]
    rank, features = a_ref.shape
    together = LANES // (2 * own)
    first = core_ref[0] == 0
    for start in range(0, z_size, together):
        pairs = [(mine_ref[z].astype(f32), got_ref[z].astype(f32)) for z in range(start, start + together)]
        gains = functools.reduce(jnp.add, [mine[2 * own :] + got[2 * own :] for mine, got in pairs])
        for y in range(2):
            lines, rows = [], slice(y * own, (y + 1) * own)
            for mine, got in pairs:
                lines += [
                    jnp.where(first, mine[rows], got[rows]),
                    jnp.where(first, got[rows], mine[rows]),
                ]
            both = jnp.concatenate(lines, axis=0).T
            place = y * (features // 2) + start * 2 * own
            a_ref[:, place : place + LANES] = both[:rank]
            b_ref[:, place : place + LANES] = both[rank:]
            gain_ref[:, place : place + LANES] = gains[y : y + 1]


def assemble(core, mine, got, rank):
    z_size, own = mine.shape[0], (mine.shape[1] - 8) // 2
    features = 2 * z_size * 2 * own
    whole = jax.ShapeDtypeStruct((rank, features), f32)
    vmem = pl.BlockSpec(memory_space=pltpu.VMEM)
    return pl.pallas_call(
        functools.partial(assemble_kernel, own),
        in_specs=[pl.BlockSpec(memory_space=pltpu.SMEM), vmem, vmem],
        out_specs=[vmem, vmem, vmem],
        out_shape=[whole, whole, jax.ShapeDtypeStruct((1, features), f32)],
        compiler_params=pltpu.CompilerParams(vmem_limit_bytes=VMEM_LIMIT),
    )(core, mine, got)


def body(resid, heads, down_matrix, up, scale, value_matrix, target):
    share, width = target.shape
    tp = resid.shape[0] // share
    tokens = resid.shape[0] * lax.axis_size(ROWS)
    rank, features = up.shape
    core = lax.axis_index("core")
    gain = scale.astype(f32)

    pieces = project(resid, heads, scale, value_matrix, down_matrix.T, up, share)
    pieces = lax.all_to_all(pieces, TP, 0, 0, tiled=True)
    values, every = owner(pieces, target, 1.0 / tokens**0.5)
    every = lax.all_to_all(every, TP, 0, 0, tiled=True)
    every = every.reshape(tp * share, -1)

    y_size, z_size, core_size = (lax.axis_size(a) for a in ("y_hi", Z, "core"))
    own = features // (y_size * z_size * core_size)
    kept, small, sent = gradients(
        core.reshape(1), every, resid.T, heads.T, up, gain[:, None], value_matrix, own, z_size
    )

    got = swap(sent, "core")
    small = small_pieces(small, got, y_size)
    small = lax.all_to_all(small, Z, 0, 0, tiled=True)

    half, got = width // 2, got[:, :, :width]
    odd, me = lax.axis_index("z_odd"), lax.axis_index("y_hi")

    def quarter(y, z):
        parts = [x.reshape(y_size, z_size, own, width) for x in (kept, got)]
        parts = [lax.dynamic_index_in_dim(x, y, 0, keepdims=False) for x in parts]
        parts = [lax.dynamic_slice_in_dim(x, z * half, half, 2) for x in parts]
        return parts[0].astype(f32) + parts[1].astype(f32)

    small, value = lax.optimization_barrier((jnp.sum(small.astype(f32), axis=0), quarter(me, odd)))
    for y, z, axis in (
        (me, 1 - odd, "z_odd"),
        (1 - me, odd, "y_hi"),
        (1 - me, 1 - odd, ("y_hi", "z_odd")),
    ):
        value = value + swap(quarter(y, z).astype(bf16), axis).astype(f32)
    value = value.astype(bf16)

    small = (small + swap(small, "y_hi")).astype(bf16)

    tiles = [value[:, :, i : i + LANES] for i in range(0, half, LANES)]
    small = jnp.broadcast_to(small, (z_size, *small.shape))
    value = lax.all_to_all(jnp.concatenate([*tiles, small], axis=1), Z, 0, 0, tiled=True)
    lines = len(tiles) * own
    small = value[:, lines:]
    a_grad, b_grad, gain_grad = assemble(core.reshape(1), small, swap(small, "core"), rank)

    value = value[:, :lines].astype(f32).reshape(-1, 2, len(tiles), own, LANES)
    value = jnp.sum(value, axis=0).transpose(2, 0, 1, 3).reshape(own, width)
    own_gain = lax.dynamic_slice_in_dim(gain, lax.axis_index(ROWS) * own, own, 0)
    value_grad = (value * own_gain[:, None]).astype(bf16)
    return (values, value_grad, a_grad.T, b_grad, gain_grad.reshape(-1))


def swap(x, axis):
    last = lax.axis_size(axis) - 1
    return lax.ppermute(x, axis, [(i, last - i) for i in range(last + 1)])


def solution(mesh):
    rows, tp = mesh.shape["rows"], mesh.shape["tp"]
    y_hi, z_odd, core, y_lo = 2, 2, 2, 2
    z_pair = rows // (y_hi * z_odd * core)
    fine = Mesh(
        mesh.devices.reshape(y_hi, z_pair, z_odd, core, tp // y_lo, y_lo), (*ROWS, *TP)
    )
    in_specs = (
        P(ROWS, TP),
        P(ROWS, TP),
        P(TP, None),
        P(None, TP),
        P(TP),
        P(TP, None),
        P((*ROWS, *TP), None),
    )
    out_specs = (
        P((*ROWS, *TP), None),
        P((*TP, *ROWS), None),
        P(TP, None),
        P(None, TP),
        P(TP),
    )
    return jax.shard_map(body, mesh=fine, in_specs=in_specs, out_specs=out_specs, check_vma=False)
```

```python
import functools

import jax
import jax.numpy as jnp
from jax import lax
from jax.experimental import pallas as pl
from jax.experimental.pallas import tpu as pltpu
from jax.sharding import Mesh, PartitionSpec as P

MODEL_WIDTH = 8192
EPSILON = 1e-06
TP = ("x", "y_lo")
Z = ("z_pair", "z_odd")
ROWS = ("y_hi", *Z, "core")
bf16 = jnp.bfloat16
f32 = jnp.float32
NN = (((1,), (0,)), ((), ()))
NT = (((1,), (1,)), ((), ()))
TN = (((0,), (0,)), ((), ()))
LANES = 128
VMEM_LIMIT = 48 * 2**20
VMEM_WHOLE = 60 * 2**20
VMEM_SOME = 16 * 2**20


def dot(a, b, dims=NN):
    return lax.dot_general(a, b, dims, preferred_element_type=f32)


def split(x):
    high = x.astype(bf16)
    return high, (x - high.astype(f32)).astype(bf16)


def dot_split(a, b, dims=NN):
    return dot(a, b[0], dims) + dot(a, b[1], dims)


def project_kernel(
    share, resid_ref, heads_ref, gain_ref, matrix_ref, down_ref, up_ref, out_ref, weights_ref
):
    rank, width = up_ref.shape[0], matrix_ref.shape[1]
    gain = gain_ref[...].astype(f32).reshape(1, -1)

    @pl.when(pl.program_id(0) == 0)
    def _():
        high, low = split(up_ref[...].astype(f32) * gain)
        weights_ref[:, :width] = dot(high, matrix_ref[...]) + dot(low, matrix_ref[...])
        gram = dot(up_ref[...], up_ref[...], NT)
        weights_ref[:, width:] = jnp.concatenate([gram, jnp.zeros_like(gram)], axis=1)

    resid = resid_ref[...]
    wide = resid.astype(f32)
    values = dot((wide * gain).astype(bf16), matrix_ref[...])
    small = [dot(heads_ref[...], down_ref[...], NT), dot(resid, up_ref[...], NT)]
    small = jnp.concatenate(small, axis=1)
    squares = jnp.sum(wide * wide, axis=1, keepdims=True)
    line = lax.broadcasted_iota(jnp.int32, (rank, share // 2), 0)
    diagonal = line[: share // 2] == lax.broadcasted_iota(jnp.int32, (share // 2, share // 2), 1)
    for piece in range(out_ref.shape[0]):
        rows = slice(piece * share, (piece + 1) * share)
        out_ref[piece, :share, :width] = values[rows].astype(bf16)
        out_ref[piece, :share, width:] = small[rows].astype(bf16)
        lines = jnp.zeros(line.shape, f32)
        for part in range(2):
            rows = slice(piece * share + part * (share // 2), piece * share + (part + 1) * (share // 2))
            across = jnp.sum(jnp.where(diagonal, squares[rows], 0.0), axis=0, keepdims=True)
            first = across.astype(bf16).astype(f32)
            lines = jnp.where(line == part, first, lines)
            lines = jnp.where(line == 2 + part, across - first, lines)
        blank = [jnp.zeros((rank, rank), f32), lines, jnp.zeros((rank, rank - share // 2), f32)]
        out_ref[piece, share:, :width] = weights_ref[:, :width].astype(bf16)
        tail = weights_ref[:, width:] + jnp.concatenate(blank, axis=1)
        out_ref[piece, share:, width:] = tail.astype(bf16)


def project(resid, heads, gain, matrix, down, up, share):
    tokens, features = resid.shape
    rank, width = up.shape[0], matrix.shape[1]
    pieces, group = tokens // share, 4
    rows, columns = group * share, width + 2 * rank
    whole = lambda i: (0, 0)
    return pl.pallas_call(
        functools.partial(project_kernel, share),
        grid=(pieces // group,),
        in_specs=[
            pl.BlockSpec((rows, features), lambda i: (i, 0)),
            pl.BlockSpec((rows, features), lambda i: (i, 0)),
            pl.BlockSpec((features,), lambda i: (0,)),
            pl.BlockSpec((features, width), whole),
            pl.BlockSpec(down.shape, whole),
            pl.BlockSpec(up.shape, whole),
        ],
        out_specs=pl.BlockSpec((group, share + rank, columns), lambda i: (i, 0, 0)),
        out_shape=jax.ShapeDtypeStruct((pieces, share + rank, columns), bf16),
        scratch_shapes=[pltpu.VMEM((rank, columns), f32)],
        compiler_params=pltpu.CompilerParams(vmem_limit_bytes=VMEM_WHOLE),
        cost_estimate=pl.CostEstimate(
            flops=2 * tokens * features * (width + 256),
            bytes_accessed=4 * tokens * features + 2 * features * width,
            transcendentals=0,
        ),
    )(resid, heads, gain, matrix, down, up)


def owner_kernel(loss_scale, pieces_ref, target_ref, values_ref, every_ref):
    share, width = target_ref.shape
    tp = pieces_ref.shape[0]
    rank = pieces_ref.shape[1] - share
    total = functools.reduce(jnp.add, [pieces_ref[i].astype(f32) for i in range(tp)])
    through = split(total[share:, :width])
    gram = split(total[share:, width : width + rank])
    lines = total[share : share + 8, width + rank : width + rank + share // 2]
    lines = lines[0:2] + lines[2:4]
    diagonal = (share // 2, share // 2)
    diagonal = lax.broadcasted_iota(jnp.int32, diagonal, 0) == lax.broadcasted_iota(jnp.int32, diagonal, 1)
    squares = jnp.concatenate(
        [
            jnp.sum(jnp.where(diagonal, lines[i : i + 1], 0.0), axis=1, keepdims=True)
            for i in range(2)
        ],
        axis=0,
    )

    down_b = total[:share, width : width + rank].astype(bf16)
    down_wide = down_b.astype(f32)
    along = total[:share, width + rank :]
    hidden_up = along + 0.5 * dot_split(down_b, gram)
    squares = squares + 0.5 * jnp.sum(down_wide * (along + hidden_up), axis=1, keepdims=True)
    inverse_rms = lax.rsqrt(squares / MODEL_WIDTH + EPSILON)
    sums = inverse_rms * (total[:share, :width] + 0.5 * dot_split(down_b, through))
    values_ref[...] = sums.astype(bf16)
    error = (sums - target_ref[...].astype(f32)) * loss_scale
    inner = jnp.sum(error * sums, axis=1, keepdims=True) / MODEL_WIDTH
    high, low = split(error)
    down_grad = dot_split(high, through, NT) + dot(low, through[0], NT)
    down_grad = 0.5 * inverse_rms * (down_grad - inner * inverse_rms * hidden_up)
    weighted = down_wide * (inner * inverse_rms * inverse_rms)
    small = jnp.concatenate([down_wide, down_grad], axis=1).astype(bf16)
    error, weighted = (error * inverse_rms).astype(bf16), weighted.astype(bf16)
    for i in range(tp):
        every_ref[i, :, :width] = error
        every_ref[i, :, width : width + 2 * rank] = small
        every_ref[i, :, width + 2 * rank :] = weighted


def owner(pieces, target, loss_scale):
    share, width = target.shape
    tp, rank = pieces.shape[0], pieces.shape[1] - share
    sent = (share, width + 3 * rank)
    vmem = pl.BlockSpec(memory_space=pltpu.VMEM)
    return pl.pallas_call(
        functools.partial(owner_kernel, loss_scale),
        in_specs=[vmem, vmem],
        out_specs=[vmem, vmem],
        out_shape=[
            jax.ShapeDtypeStruct((share, width), bf16),
            jax.ShapeDtypeStruct((tp, *sent), bf16),
        ],
        compiler_params=pltpu.CompilerParams(vmem_limit_bytes=VMEM_SOME),
    )(pieces, target)


def gradients_kernel(
    z_size, core_ref, every_ref, resid_ref, heads_ref, up_ref, gain_ref, matrix_ref,
    kept_ref, small_ref, sent_ref, cross_ref,
):
    width = matrix_ref.shape[1]
    rank = up_ref.shape[0]
    error = every_ref[:, :width]
    down = every_ref[:, width : width + rank]

    @pl.when(pl.program_id(0) == 0)
    def _():
        high, low = split(dot(error, down, TN))
        cross_ref[0] = high
        cross_ref[1] = low

    core = core_ref[0]
    matrix = matrix_ref[...]
    hidden = lax.dot_general(up_ref[...], down, (((0,), (1,)), ((), ())), preferred_element_type=f32)
    hidden = (resid_ref[...].astype(f32) + 0.5 * hidden).astype(bf16)
    value = dot(hidden, error)
    a_part = dot(heads_ref[...], every_ref[:, width + rank : width + 2 * rank])
    b_part = dot(hidden, every_ref[:, width + 2 * rank :])
    crossed = dot(matrix, cross_ref[0]) + dot(matrix, cross_ref[1])
    b_part = 0.5 * (gain_ref[...] * crossed - b_part)
    small = jnp.concatenate([a_part, b_part], axis=1)
    gain_part = jnp.sum(value * matrix.astype(f32), axis=1, keepdims=True)
    group, own = kept_ref.shape[:2]
    lane = lax.broadcasted_iota(jnp.int32, small.shape, 1)
    line = lax.rem(lax.broadcasted_iota(jnp.int32, small.shape, 0), LANES)
    spread = jnp.where(lane == line, gain_part, 0.0).reshape(2 * group, own, LANES)
    gain_line = jnp.sum(spread, axis=1, keepdims=True)
    row = lax.broadcasted_iota(jnp.int32, (2 * group, own, LANES), 1)
    piece = pl.program_id(0) * group + lax.broadcasted_iota(jnp.int32, row.shape, 0) // 2
    gain_line = jnp.where(row == piece // z_size, gain_line, 0.0)
    small = jnp.concatenate([small.reshape(2 * group, own, -1), gain_line], axis=2)
    small = small.reshape(group, 2, own, -1)
    value = value.reshape(group, 2, own, width)
    first = core == 0
    kept_ref[...] = jnp.where(first, value[:, 0], value[:, 1]).astype(bf16)
    small_ref[...] = jnp.where(first, small[:, 0], small[:, 1])
    sent_ref[:, :, :width] = jnp.where(first, value[:, 1], value[:, 0]).astype(bf16)
    sent_ref[:, :, width:] = jnp.where(first, small[:, 1], small[:, 0]).astype(bf16)


def gradients(core, every, resid, heads, up, gain, matrix, own, z_size):
    features, tokens = resid.shape
    width, rank = matrix.shape[1], up.shape[0]
    block = 512
    pieces, group = features // (2 * own), block // (2 * own)
    shapes = [
        jax.ShapeDtypeStruct((pieces, own, width), bf16),
        jax.ShapeDtypeStruct((pieces, own, 2 * rank + LANES), f32),
        jax.ShapeDtypeStruct((pieces, own, width + 2 * rank + LANES), bf16),
    ]
    return pl.pallas_call(
        functools.partial(gradients_kernel, z_size),
        grid=(features // block,),
        in_specs=[
            pl.BlockSpec(memory_space=pltpu.SMEM),
            pl.BlockSpec(every.shape, lambda i: (0, 0)),
            pl.BlockSpec((block, tokens), lambda i: (i, 0)),
            pl.BlockSpec((block, tokens), lambda i: (i, 0)),
            pl.BlockSpec((rank, block), lambda i: (0, i)),
            pl.BlockSpec((block, 1), lambda i: (i, 0)),
            pl.BlockSpec((block, width), lambda i: (i, 0)),
        ],
        out_specs=[pl.BlockSpec((group, *s.shape[1:]), lambda i: (i, 0, 0)) for s in shapes],
        out_shape=shapes,
        scratch_shapes=[pltpu.VMEM((2, width, rank), bf16)],
        compiler_params=pltpu.CompilerParams(vmem_limit_bytes=VMEM_LIMIT),
        cost_estimate=pl.CostEstimate(
            flops=2 * tokens * features * (width + 4 * rank),
            bytes_accessed=4 * tokens * features + 8 * features * width,
            transcendentals=0,
        ),
    )(core, every, resid, heads, up, gain, matrix)


def small_kernel(small_ref, got_ref, out_ref):
    z_size = out_ref.shape[0]
    y_size = small_ref.shape[0] // z_size
    small = small_ref[...] + got_ref[...].astype(f32)
    for z in range(z_size):
        places = [y * z_size + z for y in range(y_size)]
        lines = [small[i, :, :LANES] for i in places]
        gains = functools.reduce(jnp.add, [small[i, :8, LANES:] for i in places])
        out_ref[z] = jnp.concatenate([*lines, gains], axis=0).astype(bf16)


def small_pieces(small, got, y_size):
    pieces, own, columns = small.shape
    z_size = pieces // y_size
    last = got.shape[2] // columns - 1
    return pl.pallas_call(
        small_kernel,
        grid=(1,),
        in_specs=[
            pl.BlockSpec(small.shape, lambda i: (0, 0, 0)),
            pl.BlockSpec(small.shape, lambda i: (0, 0, last)),
        ],
        out_specs=pl.BlockSpec((z_size, y_size * own + 8, LANES), lambda i: (0, 0, 0)),
        out_shape=jax.ShapeDtypeStruct((z_size, y_size * own + 8, LANES), bf16),
        compiler_params=pltpu.CompilerParams(vmem_limit_bytes=VMEM_SOME),
    )(small, got)


def assemble_kernel(own, core_ref, mine_ref, got_ref, a_ref, b_ref, gain_ref):
    z_size = mine_ref.shape[0]
    rank, features = a_ref.shape
    together = LANES // (2 * own)
    first = core_ref[0] == 0
    for start in range(0, z_size, together):
        pairs = [(mine_ref[z].astype(f32), got_ref[z].astype(f32)) for z in range(start, start + together)]
        gains = functools.reduce(jnp.add, [mine[2 * own :] + got[2 * own :] for mine, got in pairs])
        for y in range(2):
            lines, rows = [], slice(y * own, (y + 1) * own)
            for mine, got in pairs:
                lines += [
                    jnp.where(first, mine[rows], got[rows]),
                    jnp.where(first, got[rows], mine[rows]),
                ]
            both = jnp.concatenate(lines, axis=0).T
            place = y * (features // 2) + start * 2 * own
            a_ref[:, place : place + LANES] = both[:rank]
            b_ref[:, place : place + LANES] = both[rank:]
            gain_ref[:, place : place + LANES] = gains[y : y + 1]


def assemble(core, mine, got, rank):
    z_size, own = mine.shape[0], (mine.shape[1] - 8) // 2
    features = 2 * z_size * 2 * own
    whole = jax.ShapeDtypeStruct((rank, features), f32)
    vmem = pl.BlockSpec(memory_space=pltpu.VMEM)
    return pl.pallas_call(
        functools.partial(assemble_kernel, own),
        in_specs=[pl.BlockSpec(memory_space=pltpu.SMEM), vmem, vmem],
        out_specs=[vmem, vmem, vmem],
        out_shape=[whole, whole, jax.ShapeDtypeStruct((1, features), f32)],
        compiler_params=pltpu.CompilerParams(vmem_limit_bytes=VMEM_LIMIT),
    )(core, mine, got)


def body(resid, heads, down_matrix, up, scale, value_matrix, target):
    share, width = target.shape
    tp = resid.shape[0] // share
    tokens = resid.shape[0] * lax.axis_size(ROWS)
    rank, features = up.shape
    core = lax.axis_index("core")
    gain = scale.astype(f32)

    pieces = project(resid, heads, scale, value_matrix, down_matrix.T, up, share)
    pieces = lax.all_to_all(pieces, TP, 0, 0, tiled=True)
    values, every = owner(pieces, target, 1.0 / tokens**0.5)
    every = lax.all_to_all(every, TP, 0, 0, tiled=True)
    every = every.reshape(tp * share, -1)

    y_size, z_size, core_size = (lax.axis_size(a) for a in ("y_hi", Z, "core"))
    own = features // (y_size * z_size * core_size)
    kept, small, sent = gradients(
        core.reshape(1), every, resid.T, heads.T, up, gain[:, None], value_matrix, own, z_size
    )

    got = swap(sent, "core")
    small = small_pieces(small, got, y_size)
    small = lax.all_to_all(small, Z, 0, 0, tiled=True)

    half, got = width // 2, got[:, :, :width]
    odd, me = lax.axis_index("z_odd"), lax.axis_index("y_hi")

    def quarter(y, z):
        parts = [x.reshape(y_size, z_size, own, width) for x in (kept, got)]
        parts = [lax.dynamic_index_in_dim(x, y, 0, keepdims=False) for x in parts]
        parts = [lax.dynamic_slice_in_dim(x, z * half, half, 2) for x in parts]
        return parts[0].astype(f32) + parts[1].astype(f32)

    own_gain = lax.dynamic_slice_in_dim(gain, lax.axis_index(ROWS) * own, own, 0)
    small, value, own_gain = lax.optimization_barrier(
        (jnp.sum(small.astype(f32), axis=0), quarter(me, odd), own_gain)
    )
    for y, z, axis in (
        (me, 1 - odd, "z_odd"),
        (1 - me, odd, "y_hi"),
        (1 - me, 1 - odd, ("y_hi", "z_odd")),
    ):
        value = value + swap(quarter(y, z).astype(bf16), axis).astype(f32)
    value = value.astype(bf16)

    small = (small + swap(small, "y_hi")).astype(bf16)

    tiles = [value[:, :, i : i + LANES] for i in range(0, half, LANES)]
    small = jnp.broadcast_to(small, (z_size, *small.shape))
    value = lax.all_to_all(jnp.concatenate([*tiles, small], axis=1), Z, 0, 0, tiled=True)
    lines = len(tiles) * own
    small = value[:, lines:]
    a_grad, b_grad, gain_grad = assemble(core.reshape(1), small, swap(small, "core"), rank)

    value = value[:, :lines].astype(f32).reshape(-1, 2, len(tiles), own, LANES)
    value = jnp.sum(value, axis=0).transpose(2, 0, 1, 3).reshape(own, width)
    value_grad = (value * own_gain[:, None]).astype(bf16)
    return (values, value_grad, a_grad.T, b_grad, gain_grad.reshape(-1))


def swap(x, axis):
    last = lax.axis_size(axis) - 1
    return lax.ppermute(x, axis, [(i, last - i) for i in range(last + 1)])


def solution(mesh):
    rows, tp = mesh.shape["rows"], mesh.shape["tp"]
    y_hi, z_odd, core, y_lo = 2, 2, 2, 2
    z_pair = rows // (y_hi * z_odd * core)
    fine = Mesh(
        mesh.devices.reshape(y_hi, z_pair, z_odd, core, tp // y_lo, y_lo), (*ROWS, *TP)
    )
    in_specs = (
        P(ROWS, TP),
        P(ROWS, TP),
        P(TP, None),
        P(None, TP),
        P(TP),
        P(TP, None),
        P((*ROWS, *TP), None),
    )
    out_specs = (
        P((*ROWS, *TP), None),
        P((*TP, *ROWS), None),
        P(TP, None),
        P(None, TP),
        P(TP),
    )
    return jax.shard_map(body, mesh=fine, in_specs=in_specs, out_specs=out_specs, check_vma=False)
```

```python
import functools

import jax
import jax.numpy as jnp
from jax import lax
from jax.experimental import pallas as pl
from jax.experimental.pallas import tpu as pltpu
from jax.sharding import Mesh, PartitionSpec as P

MODEL_WIDTH = 8192
EPSILON = 1e-06
TP = ("x", "y_lo")
Z = ("z_pair", "z_odd")
ROWS = ("y_hi", *Z, "core")
bf16 = jnp.bfloat16
f32 = jnp.float32
NN = (((1,), (0,)), ((), ()))
NT = (((1,), (1,)), ((), ()))
TN = (((0,), (0,)), ((), ()))
LANES = 128
VMEM_LIMIT = 48 * 2**20
VMEM_WHOLE = 60 * 2**20
VMEM_SOME = 16 * 2**20


def dot(a, b, dims=NN):
    return lax.dot_general(a, b, dims, preferred_element_type=f32)


def split(x):
    high = x.astype(bf16)
    return high, (x - high.astype(f32)).astype(bf16)


def dot_split(a, b, dims=NN):
    return dot(a, b[0], dims) + dot(a, b[1], dims)


def project_kernel(
    share, resid_ref, heads_ref, gain_ref, matrix_ref, down_ref, up_ref, out_ref, weights_ref
):
    rank, width = up_ref.shape[0], matrix_ref.shape[1]
    gain = gain_ref[...].astype(f32).reshape(1, -1)

    @pl.when(pl.program_id(0) == 0)
    def _():
        high, low = split(up_ref[...].astype(f32) * gain)
        weights_ref[:, :width] = dot(high, matrix_ref[...]) + dot(low, matrix_ref[...])
        gram = dot(up_ref[...], up_ref[...], NT)
        weights_ref[:, width:] = jnp.concatenate([gram, jnp.zeros_like(gram)], axis=1)

    resid = resid_ref[...]
    wide = resid.astype(f32)
    values = dot((wide * gain).astype(bf16), matrix_ref[...])
    small = [dot(heads_ref[...], down_ref[...], NT), dot(resid, up_ref[...], NT)]
    small = jnp.concatenate(small, axis=1)
    squares = jnp.sum(wide * wide, axis=1, keepdims=True)
    line = lax.broadcasted_iota(jnp.int32, (rank, share // 2), 0)
    diagonal = line[: share // 2] == lax.broadcasted_iota(jnp.int32, (share // 2, share // 2), 1)
    for piece in range(out_ref.shape[0]):
        rows = slice(piece * share, (piece + 1) * share)
        out_ref[piece, :share, :width] = values[rows].astype(bf16)
        out_ref[piece, :share, width:] = small[rows].astype(bf16)
        lines = jnp.zeros(line.shape, f32)
        for part in range(2):
            rows = slice(piece * share + part * (share // 2), piece * share + (part + 1) * (share // 2))
            across = jnp.sum(jnp.where(diagonal, squares[rows], 0.0), axis=0, keepdims=True)
            first = across.astype(bf16).astype(f32)
            lines = jnp.where(line == part, first, lines)
            lines = jnp.where(line == 2 + part, across - first, lines)
        blank = [jnp.zeros((rank, rank), f32), lines, jnp.zeros((rank, rank - share // 2), f32)]
        out_ref[piece, share:, :width] = weights_ref[:, :width].astype(bf16)
        tail = weights_ref[:, width:] + jnp.concatenate(blank, axis=1)
        out_ref[piece, share:, width:] = tail.astype(bf16)


def project(resid, heads, gain, matrix, down, up, share):
    tokens, features = resid.shape
    rank, width = up.shape[0], matrix.shape[1]
    pieces, group = tokens // share, 4
    rows, columns = group * share, width + 2 * rank
    whole = lambda i: (0, 0)
    return pl.pallas_call(
        functools.partial(project_kernel, share),
        grid=(pieces // group,),
        in_specs=[
            pl.BlockSpec((rows, features), lambda i: (i, 0)),
            pl.BlockSpec((rows, features), lambda i: (i, 0)),
            pl.BlockSpec((features,), lambda i: (0,)),
            pl.BlockSpec((features, width), whole),
            pl.BlockSpec(down.shape, whole),
            pl.BlockSpec(up.shape, whole),
        ],
        out_specs=pl.BlockSpec((group, share + rank, columns), lambda i: (i, 0, 0)),
        out_shape=jax.ShapeDtypeStruct((pieces, share + rank, columns), bf16),
        scratch_shapes=[pltpu.VMEM((rank, columns), f32)],
        compiler_params=pltpu.CompilerParams(vmem_limit_bytes=VMEM_WHOLE),
        cost_estimate=pl.CostEstimate(
            flops=2 * tokens * features * (width + 256),
            bytes_accessed=4 * tokens * features + 2 * features * width,
            transcendentals=0,
        ),
    )(resid, heads, gain, matrix, down, up)


def owner_kernel(loss_scale, pieces_ref, target_ref, values_ref, every_ref):
    share, width = target_ref.shape
    tp = pieces_ref.shape[0]
    rank = pieces_ref.shape[1] - share
    total = functools.reduce(jnp.add, [pieces_ref[i].astype(f32) for i in range(tp)])
    through = split(total[share:, :width])
    gram = split(total[share:, width : width + rank])
    lines = total[share : share + 8, width + rank : width + rank + share // 2]
    lines = lines[0:2] + lines[2:4]
    diagonal = (share // 2, share // 2)
    diagonal = lax.broadcasted_iota(jnp.int32, diagonal, 0) == lax.broadcasted_iota(jnp.int32, diagonal, 1)
    squares = jnp.concatenate(
        [
            jnp.sum(jnp.where(diagonal, lines[i : i + 1], 0.0), axis=1, keepdims=True)
            for i in range(2)
        ],
        axis=0,
    )

    down_b = total[:share, width : width + rank].astype(bf16)
    down_wide = down_b.astype(f32)
    along = total[:share, width + rank :]
    hidden_up = along + 0.5 * dot_split(down_b, gram)
    squares = squares + 0.5 * jnp.sum(down_wide * (along + hidden_up), axis=1, keepdims=True)
    inverse_rms = lax.rsqrt(squares / MODEL_WIDTH + EPSILON)
    sums = inverse_rms * (total[:share, :width] + 0.5 * dot_split(down_b, through))
    values_ref[...] = sums.astype(bf16)
    error = (sums - target_ref[...].astype(f32)) * loss_scale
    inner = jnp.sum(error * sums, axis=1, keepdims=True) / MODEL_WIDTH
    high, low = split(error)
    down_grad = dot_split(high, through, NT) + dot(low, through[0], NT)
    down_grad = 0.5 * inverse_rms * (down_grad - inner * inverse_rms * hidden_up)
    weighted = down_wide * (inner * inverse_rms * inverse_rms)
    small = jnp.concatenate([down_wide, down_grad], axis=1).astype(bf16)
    error, weighted = (error * inverse_rms).astype(bf16), weighted.astype(bf16)
    for i in range(tp):
        every_ref[i, :, :width] = error
        every_ref[i, :, width : width + 2 * rank] = small
        every_ref[i, :, width + 2 * rank :] = weighted


def owner(pieces, target, loss_scale):
    share, width = target.shape
    tp, rank = pieces.shape[0], pieces.shape[1] - share
    sent = (share, width + 3 * rank)
    vmem = pl.BlockSpec(memory_space=pltpu.VMEM)
    return pl.pallas_call(
        functools.partial(owner_kernel, loss_scale),
        in_specs=[vmem, vmem],
        out_specs=[vmem, vmem],
        out_shape=[
            jax.ShapeDtypeStruct((share, width), bf16),
            jax.ShapeDtypeStruct((tp, *sent), bf16),
        ],
        compiler_params=pltpu.CompilerParams(vmem_limit_bytes=VMEM_SOME),
    )(pieces, target)


def gradients_kernel(
    z_size, core_ref, every_ref, resid_ref, heads_ref, up_ref, gain_ref, matrix_ref,
    kept_ref, small_ref, sent_ref, cross_ref,
):
    width = matrix_ref.shape[1]
    rank = up_ref.shape[0]
    error = every_ref[:, :width]
    down = every_ref[:, width : width + rank]

    @pl.when(pl.program_id(0) == 0)
    def _():
        high, low = split(dot(error, down, TN))
        cross_ref[0] = high
        cross_ref[1] = low

    core = core_ref[0]
    matrix = matrix_ref[...]
    hidden = lax.dot_general(up_ref[...], down, (((0,), (1,)), ((), ())), preferred_element_type=f32)
    hidden = (resid_ref[...].astype(f32) + 0.5 * hidden).astype(bf16)
    value = dot(hidden, error)
    a_part = dot(heads_ref[...], every_ref[:, width + rank : width + 2 * rank])
    b_part = dot(hidden, every_ref[:, width + 2 * rank :])
    crossed = dot(matrix, cross_ref[0]) + dot(matrix, cross_ref[1])
    b_part = 0.5 * (gain_ref[...] * crossed - b_part)
    small = jnp.concatenate([a_part, b_part], axis=1)
    gain_part = jnp.sum(value * matrix.astype(f32), axis=1, keepdims=True)
    group, own = kept_ref.shape[:2]
    lane = lax.broadcasted_iota(jnp.int32, small.shape, 1)
    line = lax.rem(lax.broadcasted_iota(jnp.int32, small.shape, 0), LANES)
    spread = jnp.where(lane == line, gain_part, 0.0).reshape(2 * group, own, LANES)
    gain_line = jnp.sum(spread, axis=1, keepdims=True)
    row = lax.broadcasted_iota(jnp.int32, (2 * group, own, LANES), 1)
    piece = pl.program_id(0) * group + lax.broadcasted_iota(jnp.int32, row.shape, 0) // 2
    gain_line = jnp.where(row == piece // z_size, gain_line, 0.0)
    small = jnp.concatenate([small.reshape(2 * group, own, -1), gain_line], axis=2)
    small = small.reshape(group, 2, own, -1)
    value = value.reshape(group, 2, own, width)
    first = core == 0
    kept_ref[...] = jnp.where(first, value[:, 0], value[:, 1]).astype(bf16)
    small_ref[...] = jnp.where(first, small[:, 0], small[:, 1])
    sent_ref[:, :, :width] = jnp.where(first, value[:, 1], value[:, 0]).astype(bf16)
    sent_ref[:, :, width:] = jnp.where(first, small[:, 1], small[:, 0]).astype(bf16)


def gradients(core, every, resid, heads, up, gain, matrix, own, z_size):
    features, tokens = resid.shape
    width, rank = matrix.shape[1], up.shape[0]
    block = 512
    pieces, group = features // (2 * own), block // (2 * own)
    shapes = [
        jax.ShapeDtypeStruct((pieces, own, width), bf16),
        jax.ShapeDtypeStruct((pieces, own, 2 * rank + LANES), f32),
        jax.ShapeDtypeStruct((pieces, own, width + 2 * rank + LANES), bf16),
    ]
    return pl.pallas_call(
        functools.partial(gradients_kernel, z_size),
        grid=(features // block,),
        in_specs=[
            pl.BlockSpec(memory_space=pltpu.SMEM),
            pl.BlockSpec(every.shape, lambda i: (0, 0)),
            pl.BlockSpec((block, tokens), lambda i: (i, 0)),
            pl.BlockSpec((block, tokens), lambda i: (i, 0)),
            pl.BlockSpec((rank, block), lambda i: (0, i)),
            pl.BlockSpec((block, 1), lambda i: (i, 0)),
            pl.BlockSpec((block, width), lambda i: (i, 0)),
        ],
        out_specs=[pl.BlockSpec((group, *s.shape[1:]), lambda i: (i, 0, 0)) for s in shapes],
        out_shape=shapes,
        scratch_shapes=[pltpu.VMEM((2, width, rank), bf16)],
        compiler_params=pltpu.CompilerParams(vmem_limit_bytes=VMEM_LIMIT),
        cost_estimate=pl.CostEstimate(
            flops=2 * tokens * features * (width + 4 * rank),
            bytes_accessed=4 * tokens * features + 8 * features * width,
            transcendentals=0,
        ),
    )(core, every, resid, heads, up, gain, matrix)


def small_kernel(small_ref, got_ref, out_ref):
    z_size = out_ref.shape[0]
    y_size = small_ref.shape[0] // z_size
    small = small_ref[...] + got_ref[...].astype(f32)
    for z in range(z_size):
        places = [y * z_size + z for y in range(y_size)]
        lines = [small[i, :, :LANES] for i in places]
        gains = functools.reduce(jnp.add, [small[i, :8, LANES:] for i in places])
        out_ref[z] = jnp.concatenate([*lines, gains], axis=0).astype(bf16)


def small_pieces(small, got, y_size):
    pieces, own, columns = small.shape
    z_size = pieces // y_size
    last = got.shape[2] // columns - 1
    return pl.pallas_call(
        small_kernel,
        grid=(1,),
        in_specs=[
            pl.BlockSpec(small.shape, lambda i: (0, 0, 0)),
            pl.BlockSpec(small.shape, lambda i: (0, 0, last)),
        ],
        out_specs=pl.BlockSpec((z_size, y_size * own + 8, LANES), lambda i: (0, 0, 0)),
        out_shape=jax.ShapeDtypeStruct((z_size, y_size * own + 8, LANES), bf16),
        compiler_params=pltpu.CompilerParams(vmem_limit_bytes=VMEM_SOME),
    )(small, got)


def assemble_kernel(own, core_ref, mine_ref, got_ref, a_ref, b_ref, gain_ref):
    z_size = mine_ref.shape[0]
    rank, features = a_ref.shape
    together = LANES // (2 * own)
    first = core_ref[0] == 0
    for start in range(0, z_size, together):
        pairs = [(mine_ref[z].astype(f32), got_ref[z].astype(f32)) for z in range(start, start + together)]
        gains = functools.reduce(jnp.add, [mine[2 * own :] + got[2 * own :] for mine, got in pairs])
        for y in range(2):
            lines, rows = [], slice(y * own, (y + 1) * own)
            for mine, got in pairs:
                lines += [
                    jnp.where(first, mine[rows], got[rows]),
                    jnp.where(first, got[rows], mine[rows]),
                ]
            both = jnp.concatenate(lines, axis=0).T
            place = y * (features // 2) + start * 2 * own
            a_ref[:, place : place + LANES] = both[:rank]
            b_ref[:, place : place + LANES] = both[rank:]
            gain_ref[:, place : place + LANES] = gains[y : y + 1]


def assemble(core, mine, got, rank):
    z_size, own = mine.shape[0], (mine.shape[1] - 8) // 2
    features = 2 * z_size * 2 * own
    whole = jax.ShapeDtypeStruct((rank, features), f32)
    vmem = pl.BlockSpec(memory_space=pltpu.VMEM)
    return pl.pallas_call(
        functools.partial(assemble_kernel, own),
        in_specs=[pl.BlockSpec(memory_space=pltpu.SMEM), vmem, vmem],
        out_specs=[vmem, vmem, vmem],
        out_shape=[whole, whole, jax.ShapeDtypeStruct((1, features), f32)],
        compiler_params=pltpu.CompilerParams(vmem_limit_bytes=VMEM_LIMIT),
    )(core, mine, got)


def body(resid, heads, down_matrix, up, scale, value_matrix, target):
    share, width = target.shape
    tp = resid.shape[0] // share
    tokens = resid.shape[0] * lax.axis_size(ROWS)
    rank, features = up.shape
    core = lax.axis_index("core")
    gain = scale.astype(f32)

    pieces = project(resid, heads, scale, value_matrix, down_matrix.T, up, share)
    pieces = lax.all_to_all(pieces, TP, 0, 0, tiled=True)
    values, every = owner(pieces, target, 1.0 / tokens**0.5)
    every = lax.all_to_all(every, TP, 0, 0, tiled=True)
    every = every.reshape(tp * share, -1)

    y_size, z_size, core_size = (lax.axis_size(a) for a in ("y_hi", Z, "core"))
    own = features // (y_size * z_size * core_size)
    kept, small, sent = gradients(
        core.reshape(1), every, resid.T, heads.T, up, gain[:, None], value_matrix, own, z_size
    )

    got = swap(sent, "core")
    small = small_pieces(small, got, y_size)
    small = lax.all_to_all(small, Z, 0, 0, tiled=True)

    half, got = width // 2, got[:, :, :width]
    odd, me = lax.axis_index("z_odd"), lax.axis_index("y_hi")

    def quarter(y, z):
        parts = [x.reshape(y_size, z_size, own, width) for x in (kept, got)]
        parts = [lax.dynamic_index_in_dim(x, y, 0, keepdims=False) for x in parts]
        parts = [lax.dynamic_slice_in_dim(x, z * half, half, 2) for x in parts]
        return parts[0].astype(f32) + parts[1].astype(f32)

    own_gain = lax.dynamic_slice_in_dim(gain, lax.axis_index(ROWS) * own, own, 0)
    small, value, own_gain = lax.optimization_barrier(
        (jnp.sum(small.astype(f32), axis=0), quarter(me, odd), own_gain)
    )
    for y, z, axis in (
        (1 - me, 1 - odd, ("y_hi", "z_odd")),
        (me, 1 - odd, "z_odd"),
        (1 - me, odd, "y_hi"),
    ):
        value = value + swap(quarter(y, z).astype(bf16), axis).astype(f32)
    value = value.astype(bf16)

    small = (small + swap(small, "y_hi")).astype(bf16)

    tiles = [value[:, :, i : i + LANES] for i in range(0, half, LANES)]
    small = jnp.broadcast_to(small, (z_size, *small.shape))
    value = lax.all_to_all(jnp.concatenate([*tiles, small], axis=1), Z, 0, 0, tiled=True)
    lines = len(tiles) * own
    small = value[:, lines:]
    a_grad, b_grad, gain_grad = assemble(core.reshape(1), small, swap(small, "core"), rank)

    value = value[:, :lines].astype(f32).reshape(-1, 2, len(tiles), own, LANES)
    value = jnp.sum(value, axis=0).transpose(2, 0, 1, 3).reshape(own, width)
    value_grad = (value * own_gain[:, None]).astype(bf16)
    return (values, value_grad, a_grad.T, b_grad, gain_grad.reshape(-1))


def swap(x, axis):
    last = lax.axis_size(axis) - 1
    return lax.ppermute(x, axis, [(i, last - i) for i in range(last + 1)])


def solution(mesh):
    rows, tp = mesh.shape["rows"], mesh.shape["tp"]
    y_hi, z_odd, core, y_lo = 2, 2, 2, 2
    z_pair = rows // (y_hi * z_odd * core)
    fine = Mesh(
        mesh.devices.reshape(y_hi, z_pair, z_odd, core, tp // y_lo, y_lo), (*ROWS, *TP)
    )
    in_specs = (
        P(ROWS, TP),
        P(ROWS, TP),
        P(TP, None),
        P(None, TP),
        P(TP),
        P(TP, None),
        P((*ROWS, *TP), None),
    )
    out_specs = (
        P((*ROWS, *TP), None),
        P((*TP, *ROWS), None),
        P(TP, None),
        P(None, TP),
        P(TP),
    )
    return jax.shard_map(body, mesh=fine, in_specs=in_specs, out_specs=out_specs, check_vma=False)
```
